32 devices in a mesh: sub: 8 (over z, x), site: 4 (over y, core).
Axes of the slice: x: 2, y: 2, z: 4, core: 2. Of those that a mesh axis runs over, the one named last changes fastest.
Arguments:
- sgt: bfloat16 [128, 2, 2, 6, 64, 128], P('sub', None, None, None, 'site'), may hold values from -6 to 6
- mechanism: float32 [128, 6], P('sub'), may hold values from -5 to 5
- slip: bfloat16 [128, 64, 2, 128], P('sub'), may hold values from -0.3125 to 0.3125
- point_list: int32 [128], replicated, may hold values from 0 to 127, as said below
- subfault_counts: int32 [8], replicated, may hold values from 1 to 16, 64 in all
Outputs:
- seismograms: bfloat16 [64, 2, 64, 2048], P('sub', None, 'site')
- psa: float32 [64, 2, 64, 40], P('sub', None, 'site')
The draws below stay inside these ranges and needn't reach their ends.
Inputs may be any that keep to these rules, and one draw needn't show every extreme that they name: `point_list`: every SGT point is named by exactly one subfault slot. Of the 16 slots of each worker w (slots w * 16 to w * 16 + 15), exactly 2 name points of each reader block r (points r * 16 to r * 16 + 15). `subfault_counts`: the counts sum to 64, and the largest is 16. Slots of a worker past its count are not part of the rupture.
All inputs are finite; a program needn't handle non-finite values.
Results may differ from the reference program's by a relative error of at most 0.0049.
Values may be sent and summed in bfloat16 or wider, within the bound.
No kernel may reach another device: no remote copies, remote signals or barrier semaphores. Data moves between devices by JAX's collectives and lax.ppermute only.
A program may use at most 128 MiB of HBM per device.

```python
import math
import jax
import jax.numpy as jnp
import numpy as np
from jax import lax

NT = 2048
FREQS = 128
VARS = 64
PERIODS = 40
CAP = 2
WORKERS = 8
SLOTS = 16
PT_DEV = 16
SUBFAULTS = 128
POINTS = 128
SITES = 64


def draw_point_list(key, part):
    reader_key, row_key = jax.random.split(key)
    base_readers = jnp.repeat(jnp.arange(WORKERS, dtype=jnp.int32), CAP)
    tiled_ids = jnp.tile(base_readers[None, :], (WORKERS, 1))
    readers = jax.random.permutation(reader_key, tiled_ids, axis=1, independent=True)
    onehot = (readers[:, :, None] == jnp.arange(WORKERS, dtype=jnp.int32)[None, None, :]).astype(jnp.int32)
    occurrence = jnp.sum(onehot * jnp.cumsum(onehot, axis=1), axis=2) - 1
    base_rows = jnp.tile(jnp.arange(PT_DEV, dtype=jnp.int32)[None, :], (WORKERS, 1))
    row_perm = jax.random.permutation(row_key, base_rows, axis=1, independent=True)
    request = jnp.arange(WORKERS, dtype=jnp.int32)[:, None] * CAP + occurrence
    row_ids = row_perm[readers, request]
    return (readers * PT_DEV + row_ids).reshape(-1).astype(jnp.int32)


def raised(result, stream_key, source, target, blocks, factor):
    def block_of(dim):
        return (jnp.arange(result.shape[dim]) // (result.shape[dim] // blocks)).reshape((-1,) + (1,) * (result.ndim - 1 - dim))

    near = jax.random.permutation(stream_key, blocks)[block_of(target)]
    second = (block_of(target) + blocks // 2) % blocks
    return jnp.where((block_of(source) == near) | (block_of(source) == second), factor * result, result)


def levels(rng, dims, shards, least, largest):
    level, own = 1.0, jax.random.fold_in(rng, 6)
    for position, blocks in shards:
        heights = jnp.exp(jax.random.uniform(jax.random.fold_in(own, position), (blocks,), jnp.float32, least / len(shards), largest / len(shards)))
        level = level * jnp.repeat(heights, dims[position] // blocks).reshape([-1 if axis == position else 1 for axis in range(len(dims))])
    return level


def split_up(amount, total, most, slope):
    loads = [(1 << 20) // math.isqrt(rank ** slope) + 1 for rank in range(2, amount + 1)]
    rest, counts = total - most - (amount - 1), [1] * (amount - 1)
    while rest > 0:
        candidates = [i for i in range(amount - 1) if counts[i] < most]
        mass, budget = sum([loads[i] for i in candidates]), rest
        for i in candidates:
            extra = min(most - counts[i], max(1, budget * loads[i] // mass), rest)
            counts[i] = counts[i] + extra
            rest = rest - extra
    return np.array([most] + counts)


def uneven_parts(stream_key, number_of, total, reach, slope):
    if number_of == 2:
        one = jax.random.randint(stream_key, (), max(1, total - reach), min(reach, total - 1) + 1)
        return jnp.stack([one, total - one])
    lengths = jnp.asarray(split_up(number_of, total, reach, slope), jnp.int32)
    pairs = (number_of - 1) // 2
    source_of, sink = lengths[1:1 + 2 * pairs:2], lengths[2:2 + 2 * pairs:2]
    margin = jnp.minimum(source_of - 1, reach - sink)
    shifted = jax.random.randint(jax.random.fold_in(stream_key, 1), (pairs,), 0, 1 << 20) % (margin + 1)
    lengths = lengths.at[1:1 + 2 * pairs:2].set(source_of - shifted).at[2:2 + 2 * pairs:2].set(sink + shifted)
    return lengths[jax.random.permutation(jax.random.fold_in(stream_key, 2), number_of)]


def gaussian(stream_key, extent, spread, bound, cuts=(), kind=jnp.bfloat16):
    result = spread * jax.random.normal(stream_key, extent, jnp.float32)
    if cuts:
        result = result * levels(stream_key, extent, cuts, -0.22, 0.18)
    return jnp.clip(result, -bound, bound).astype(kind)


def gaussian_with(stream_key, extent, scale, reach, cuts, heavy, kind=jnp.bfloat16):
    values = scale * jax.random.normal(stream_key, extent, jnp.float32)
    if cuts:
        values = values * levels(stream_key, extent, cuts, -0.22, 0.18)
    return jnp.clip(raised(values, jax.random.fold_in(stream_key, 3), *heavy), -reach, reach).astype(kind)


def setup_inputs(seed: int = 0) -> dict:
    key_list = jax.random.split(jax.random.key(seed), 6)
    return {
        "sgt": gaussian(key_list[0], (POINTS, 2, 2, 6, SITES, FREQS), 1.0, 6.0, ((0, 8), (4, 4))),
        "mechanism": gaussian(key_list[1], (SUBFAULTS, 6), 1.0, 5.0, ((0, 8),), jnp.float32),
        "slip": gaussian_with(key_list[2], (SUBFAULTS, VARS, 2, FREQS), (6 * SUBFAULTS) ** -0.5, 0.3125, ((0, 8),), (0, 1, 8, 2.0)),
        "point_list": draw_point_list(jax.random.fold_in(key_list[5], 71), 0),
        "subfault_counts": uneven_parts(key_list[4], WORKERS, SUBFAULTS // 2, SLOTS, 2).astype(jnp.int32),
    }


damping = 0.05
sample_step = 0.1

def synthesis_basis(freq_count, sample_count):
    freq_ids = jnp.arange(freq_count, dtype=jnp.int32)
    time_ids = jnp.arange(sample_count, dtype=jnp.int32)
    angles = (freq_ids[:, None] * time_ids[None, :] % sample_count).astype(jnp.float32) * (2.0 * math.pi / sample_count)
    norm_scale = 1.0 / math.sqrt(freq_count)
    return jnp.stack([norm_scale * jnp.cos(angles), -norm_scale * jnp.sin(angles)])

def oscillator_gains(period_count, freq_count, sample_count):
    period_ids = jnp.arange(period_count, dtype=jnp.float32)
    periods = 2.0 * jnp.exp(period_ids * (math.log(5.0) / max(period_count - 1, 1)))
    natural = 2.0 * math.pi / periods
    omega_bins = jnp.arange(freq_count, dtype=jnp.float32) * (2.0 * math.pi / (sample_count * sample_step))
    squared_natural = (natural * natural)[:, None]
    real_part = squared_natural - (omega_bins * omega_bins)[None, :]
    imag_part = 2.0 * damping * natural[:, None] * omega_bins[None, :]
    magnitude = real_part * real_part + imag_part * imag_part
    return (-squared_natural * real_part / magnitude, squared_natural * imag_part / magnitude)

def reference(sgt, mechanism, slip, point_list, subfault_counts):
    slot_ids = jnp.arange(SUBFAULTS, dtype=jnp.int32)
    owner_ids = slot_ids // SLOTS
    valid_mask = slot_ids % SLOTS < jnp.take(subfault_counts, owner_ids)
    slip_live = slip * valid_mask.astype(slip.dtype)[:, None, None, None]

    def add_block(running, block_index):
        block_start = block_index * SLOTS
        point_rows = lax.dynamic_slice_in_dim(point_list, block_start, SLOTS)
        green_rows = jnp.take(sgt, point_rows, axis=0).astype(jnp.float32)
        moments = lax.dynamic_slice_in_dim(mechanism, block_start, SLOTS)
        combined = moments[:, 0, None, None, None, None] * green_rows[:, :, :, 0]
        for strain in range(1, 6):
            combined = combined + moments[:, strain, None, None, None, None] * green_rows[:, :, :, strain]
        projected = lax.optimization_barrier(combined.astype(jnp.bfloat16)).astype(jnp.float32)
        slip_block = lax.dynamic_slice_in_dim(slip_live, block_start, SLOTS).astype(jnp.float32)
        with_real = jnp.einsum('jrcsf,jvf->rvcsf', projected, slip_block[:, :, 0], precision=lax.Precision.HIGHEST)
        with_imag = jnp.einsum('jrcsf,jvf->rvcsf', projected, slip_block[:, :, 1], precision=lax.Precision.HIGHEST)
        update = jnp.stack([with_real[0] - with_imag[1], with_imag[0] + with_real[1]], axis=2)
        return (running + update, None)
    start_value = jnp.zeros((VARS, 2, 2, SITES, FREQS), jnp.float32)
    spectrum = lax.scan(add_block, start_value, jnp.arange(WORKERS, dtype=jnp.int32))[0]
    basis = synthesis_basis(FREQS, NT)
    motion = jnp.einsum('vcrsf,rft->vcst', spectrum, basis, precision=lax.Precision.HIGHEST)
    seismograms = motion.astype(jnp.bfloat16)
    gain_real, gain_imag = oscillator_gains(PERIODS, FREQS, NT)
    basis_low = lax.optimization_barrier(basis.astype(jnp.bfloat16)).astype(jnp.float32)
    spec_real = spectrum[:, :, 0]
    spec_imag = spectrum[:, :, 1]

    def one_period(gains):
        resp_real = gains[0] * spec_real - gains[1] * spec_imag
        resp_imag = gains[0] * spec_imag + gains[1] * spec_real
        response = jnp.stack([resp_real, resp_imag], axis=2).astype(jnp.bfloat16)
        response = lax.optimization_barrier(response).astype(jnp.float32)
        response_wave = jnp.einsum('vcrsf,rft->vcst', response, basis_low, precision=lax.Precision.HIGHEST)
        return lax.optimization_barrier(jnp.max(jnp.abs(response_wave), axis=3))
    peak_values = lax.map(one_period, jnp.stack([gain_real, gain_imag], axis=1))
    return (seismograms, jnp.transpose(peak_values, (1, 2, 3, 0)))
```

```python
import functools
import math

import jax
import jax.numpy as jnp
from jax import lax
from jax.experimental import pallas as pl
from jax.experimental.pallas import tpu as pltpu
from jax.sharding import PartitionSpec as P

NT = 2048
PERIODS = 40

damping = 0.05
sample_step = 0.1

LANES = 128
STRAINS = 6
BF16 = jnp.bfloat16
F32 = jnp.float32


def synthesis_basis(freq_count, sample_count):
    freq_ids = jnp.arange(freq_count, dtype=jnp.int32)
    time_ids = jnp.arange(sample_count, dtype=jnp.int32)
    angles = (time_ids[:, None] * freq_ids[None, :] % sample_count).astype(F32) * (
        2.0 * math.pi / sample_count
    )
    norm_scale = 1.0 / math.sqrt(freq_count)
    return jnp.concatenate([norm_scale * jnp.cos(angles), -norm_scale * jnp.sin(angles)], axis=1)


def oscillator_gains(period_count, freq_count, sample_count):
    period_ids = jnp.arange(period_count, dtype=F32)
    periods = 2.0 * jnp.exp(period_ids * (math.log(5.0) / max(period_count - 1, 1)))
    natural = 2.0 * math.pi / periods
    omega_bins = jnp.arange(freq_count, dtype=F32) * (2.0 * math.pi / (sample_count * sample_step))
    squared_natural = (natural * natural)[:, None]
    real_part = squared_natural - (omega_bins * omega_bins)[None, :]
    imag_part = 2.0 * damping * natural[:, None] * omega_bins[None, :]
    magnitude = real_part * real_part + imag_part * imag_part
    return (-squared_natural * real_part / magnitude, squared_natural * imag_part / magnitude)


def swap_blocks(parts):
    count = len(parts)
    width = LANES // count
    parts = list(parts)
    group = lax.broadcasted_iota(jnp.int32, parts[0].shape, 1) // width
    step = 1
    while step < count:
        low_lanes = (group & step) == 0
        for x in range(count):
            if x & step:
                continue
            low, high = parts[x], parts[x | step]
            parts[x] = jnp.where(low_lanes, low, pltpu.roll(high, width * step, 1))
            parts[x | step] = jnp.where(low_lanes, pltpu.roll(low, LANES - width * step, 1), high)
        step *= 2
    return parts


def spread_groups(packed, count):
    width = LANES // count
    group = lax.broadcasted_iota(jnp.int32, packed.shape, 1) // width
    arrays = [packed]
    step = count // 2
    while step:
        low_lanes = (group & step) == 0
        split = []
        for array in arrays:
            other = pltpu.roll(array, width * step, 1) if 2 * width * step == LANES else None
            if other is None:
                up = pltpu.roll(array, width * step, 1)
                down = pltpu.roll(array, LANES - width * step, 1)
            else:
                up = down = other
            split.append(jnp.where(low_lanes, array, up))
            split.append(jnp.where(low_lanes, down, array))
        arrays = split
        step //= 2
    return arrays


def pack_slip_kernel(workers, slip_ref, mech_ref, out_ref, wide, padded):
    core = lax.rem(lax.axis_index("site"), 2)
    stride = 2 * workers
    rows = slip_ref.shape[0] // stride
    chunk = 16
    wide[...] = slip_ref[...].astype(F32)
    for start in range(0, rows, chunk):
        parts = [
            wide[pl.ds(start * stride + 2 * x + core, chunk, stride=stride), :]
            for x in range(workers)
        ]
        for d, part in enumerate(swap_blocks(parts)):
            out_ref[d, start : start + chunk, :] = part.astype(BF16)
    padded[...] = jnp.zeros_like(padded)
    padded[:, :STRAINS] = mech_ref[...]
    moments = padded[...]
    first = moments.astype(BF16).astype(F32)
    second = (moments - first).astype(BF16).astype(F32)
    third = moments - first - second
    coded = (
        first + pltpu.roll(second, STRAINS, 1) + pltpu.roll(third, 2 * STRAINS, 1)
    ).astype(BF16)
    for d in range(workers):
        out_ref[d, rows:, :] = coded


def project_kernel(workers, point_ref, sgt_ref, recv_ref, out_ref, slot_of, moments, wide):
    me = lax.axis_index("sub")
    points = sgt_ref.shape[0]
    sites = sgt_ref.shape[4]
    total = point_ref.shape[0]
    slots = total // workers
    mech_start = recv_ref.shape[1] - slots

    def note_slot(j, carry):
        slot_of[point_ref[j]] = j
        return carry

    lax.fori_loop(0, total, note_slot, 0, unroll=8)
    for w in range(workers):
        coded = recv_ref[w, mech_start:, :].astype(F32)
        moments[w * slots : (w + 1) * slots, :] = (
            coded
            + pltpu.roll(coded, LANES - STRAINS, 1)
            + pltpu.roll(coded, LANES - 2 * STRAINS, 1)
        )
    height = 4 * sites

    def one_point(row, carry):
        moment = moments[pl.ds(slot_of[me * points + row], 1), :]
        weights = [
            jnp.broadcast_to(moment[:, m : m + 1], (sites, LANES)) for m in range(STRAINS)
        ]
        for p in range(2):
            for c in range(2):
                combined = weights[0] * sgt_ref[row, p, c, 0].astype(F32)
                for m in range(1, STRAINS):
                    combined = combined + weights[m] * sgt_ref[row, p, c, m].astype(F32)
                start = pl.multiple_of(row * height + (2 * p + c) * sites, sites)
                wide[pl.ds(start, sites), :] = combined.astype(BF16).astype(F32)
        return carry

    lax.fori_loop(0, points, one_point, 0, unroll=2)
    rows = out_ref.shape[1]
    chunk = 16
    for start in range(0, rows, chunk):
        parts = [
            wide[pl.ds(start * workers + x, chunk, stride=workers), :] for x in range(workers)
        ]
        for d, part in enumerate(swap_blocks(parts)):
            out_ref[d, start : start + chunk, :] = part.astype(BF16)


def contract_kernel(
    workers, point_ref, count_ref, own_ref, other_ref, proj_ref, out_ref, live, slip, proj, total
):
    core = lax.rem(lax.axis_index("site"), 2)
    slots = point_ref.shape[0] // workers
    slip_rows = own_ref.shape[1] - slots
    tall = slip_rows // slots
    proj_rows = proj_ref.shape[1]
    high = proj_rows // slots
    half = high // 2
    block = 4

    def note_worker(w, filled):
        def note_slot(k, carry):
            live[filled + k] = w * slots + k
            return carry

        count = count_ref[w]
        lax.fori_loop(0, count, note_slot, 0)
        return filled + count

    amount = lax.fori_loop(0, workers, note_worker, 0)
    for w in range(workers):
        slip[core, w * slip_rows : (w + 1) * slip_rows, :] = own_ref[w, :slip_rows, :].astype(F32)
        slip[1 - core, w * slip_rows : (w + 1) * slip_rows, :] = other_ref[
            w, :slip_rows, :
        ].astype(F32)
        proj[w * proj_rows : (w + 1) * proj_rows, :] = proj_ref[w].astype(F32)
    total[...] = jnp.zeros_like(total)
    lines = min(2, half)

    def add_slots(first, number):
        slots_here = [live[first + i] for i in range(number)]
        spread = [
            [
                spread_groups(slip[p, pl.ds(pl.multiple_of(j * tall, tall), tall), :], workers)
                for p in range(2)
            ]
            for j in slots_here
        ]
        starts = [point_ref[j] * high for j in slots_here]
        for line in range(0, half, lines):
            for x in range(workers):
                for y in range(line, line + lines):
                    where_real = (y * workers + x) * tall
                    where_imag = ((half + y) * workers + x) * tall
                    real = total[where_real : where_real + tall, :]
                    imag = total[where_imag : where_imag + tall, :]
                    for i in range(number):
                        green_real = proj[pl.ds(starts[i] + y, 1), :]
                        green_imag = proj[pl.ds(starts[i] + half + y, 1), :]
                        slip_real, slip_imag = spread[i][0][x], spread[i][1][x]
                        real = real + (green_real * slip_real - green_imag * slip_imag)
                        imag = imag + (green_real * slip_imag + green_imag * slip_real)
                    total[where_real : where_real + tall, :] = real
                    total[where_imag : where_imag + tall, :] = imag

    def add_block(i, carry):
        add_slots(i * block, block)
        return carry

    def add_one(i, carry):
        add_slots(i, 1)
        return carry

    lax.fori_loop(0, amount // block, add_block, 0)
    lax.fori_loop((amount // block) * block, amount, add_one, 0)
    variations = workers * tall
    for d in range(workers):
        for v in range(tall):
            y, x = divmod(d * tall + v, workers)
            out_ref[d, v * high : (v + 1) * high, :] = total[
                pl.ds(x * tall + y, high, stride=variations), :
            ]


def dot_rows(a, b):
    return lax.dot_general(a, b, (((1,), (1,)), ((), ())), preferred_element_type=F32)


def synthesis_kernel(
    workers,
    tall,
    recv_ref,
    gain_re_ref,
    gain_im_ref,
    basis_ref,
    rest_ref,
    motion_ref,
    peak_ref,
    natural,
    peaks,
):
    rows = recv_ref.shape[1]
    for x, part in enumerate(swap_blocks([recv_ref[w] for w in range(workers)])):
        natural[pl.ds(x, rows, stride=workers), :] = part
    freqs = natural.shape[1]
    width = natural.shape[0] // (2 * tall)
    real = jnp.concatenate(
        [natural[(2 * v) * width : (2 * v + 1) * width, :] for v in range(tall)], axis=0
    )
    imag = jnp.concatenate(
        [natural[(2 * v + 1) * width : (2 * v + 2) * width, :] for v in range(tall)], axis=0
    )
    real_main, imag_main = real.astype(BF16), imag.astype(BF16)
    main = jnp.concatenate([real_main, imag_main], axis=1)
    rest = jnp.concatenate(
        [
            (real - real_main.astype(F32)).astype(BF16),
            (imag - imag_main.astype(F32)).astype(BF16),
        ],
        axis=1,
    )
    samples = basis_ref.shape[0]
    tile = 256
    for t in range(0, samples, tile):
        motion = dot_rows(main, basis_ref[t : t + tile, :])
        motion = motion + dot_rows(rest, basis_ref[t : t + tile, :])
        motion = motion + dot_rows(main, rest_ref[t : t + tile, :])
        motion_ref[:, t : t + tile] = motion.astype(BF16)
    tile = 512

    def one_period(q):
        gain_re = gain_re_ref[pl.ds(q, 1), :]
        gain_im = gain_im_ref[pl.ds(q, 1), :]
        response = jnp.concatenate(
            [
                (gain_re * real - gain_im * imag).astype(BF16),
                (gain_re * imag + gain_im * real).astype(BF16),
            ],
            axis=1,
        )
        peak = None
        for t in range(0, samples, tile):
            wave = jnp.abs(dot_rows(basis_ref[t : t + tile, :], response))
            wave = jnp.max(wave.reshape(tile // 8, 8, wave.shape[1]), axis=0)
            peak = wave if peak is None else jnp.maximum(peak, wave)
        peaks[pl.ds(q, 1), :] = jnp.max(peak, axis=0, keepdims=True)

    periods = gain_re_ref.shape[0]
    group = 20

    def some_periods(i, carry):
        for u in range(group):
            one_period(i * group + u)
        return carry

    lax.fori_loop(0, periods // group, some_periods, 0)
    for q in range(periods - periods % group, periods):
        one_period(q)
    peak_ref[...] = peaks[...].T[:, :periods]


def vmem():
    return pl.BlockSpec(memory_space=pltpu.VMEM)


def smem():
    return pl.BlockSpec(memory_space=pltpu.SMEM)


def params(mebibytes):
    return pltpu.CompilerParams(vmem_limit_bytes=mebibytes * 2**20)


def per_device(sgt, mechanism, slip, point_list, subfault_counts):
    workers = lax.axis_size("sub")
    site_parts = lax.axis_size("site")
    slots, variations, _, freqs = slip.shape
    points, _, components, _, sites, _ = sgt.shape
    total = point_list.shape[0]
    tall = variations // workers
    high = 2 * components * sites // workers
    slip_rows = slots * tall
    proj_rows = points * high
    flat = slip.reshape(slots * variations * 2, freqs)
    packed = pl.pallas_call(
        functools.partial(pack_slip_kernel, workers),
        out_shape=jax.ShapeDtypeStruct((workers, slip_rows + slots, LANES), BF16),
        in_specs=[vmem(), vmem()],
        out_specs=vmem(),
        scratch_shapes=[pltpu.VMEM(flat.shape, F32), pltpu.VMEM((slots, LANES), F32)],
        compiler_params=params(16),
        name="pack_slip",
    )(flat, mechanism)
    own = lax.all_to_all(packed, "sub", split_axis=0, concat_axis=0, tiled=True)
    other = lax.ppermute(own, "site", [(i, i ^ 1) for i in range(site_parts)])
    projected = pl.pallas_call(
        functools.partial(project_kernel, workers),
        out_shape=jax.ShapeDtypeStruct((workers, proj_rows, LANES), BF16),
        in_specs=[smem(), vmem(), vmem()],
        out_specs=vmem(),
        scratch_shapes=[
            pltpu.SMEM((total,), jnp.int32),
            pltpu.VMEM((total, LANES), F32),
            pltpu.VMEM((proj_rows * workers, LANES), F32),
        ],
        compiler_params=params(24),
        name="project",
    )(point_list, sgt, own)
    chunks = lax.all_to_all(projected, "sub", split_axis=0, concat_axis=0, tiled=True)
    partial_rows = tall * high
    spectrum = pl.pallas_call(
        functools.partial(contract_kernel, workers),
        out_shape=jax.ShapeDtypeStruct((workers, partial_rows, LANES), F32),
        in_specs=[smem(), smem(), vmem(), vmem(), vmem()],
        out_specs=vmem(),
        scratch_shapes=[
            pltpu.SMEM((total,), jnp.int32),
            pltpu.VMEM((2, workers * slip_rows, LANES), F32),
            pltpu.VMEM((workers * proj_rows, LANES), F32),
            pltpu.VMEM((high * variations, LANES), F32),
        ],
        compiler_params=params(24),
        name="contract",
    )(point_list, subfault_counts, own, other, chunks)
    spectrum = lax.all_to_all(spectrum, "sub", split_axis=0, concat_axis=0, tiled=True)
    basis = synthesis_basis(freqs, NT)
    basis_low = basis.astype(BF16)
    basis_rest = (basis - lax.reduce_precision(basis, 8, 7)).astype(BF16)
    gain_re, gain_im = oscillator_gains(PERIODS, freqs, NT)
    width = tall * components * sites
    motion, peaks = pl.pallas_call(
        functools.partial(synthesis_kernel, workers, tall),
        out_shape=(
            jax.ShapeDtypeStruct((width, NT), BF16),
            jax.ShapeDtypeStruct((width, PERIODS), F32),
        ),
        in_specs=[vmem()] * 5,
        out_specs=(vmem(), vmem()),
        scratch_shapes=[
            pltpu.VMEM((2 * width, freqs), F32),
            pltpu.VMEM((LANES, width), F32),
        ],
        compiler_params=params(32),
        name="synthesis",
    )(spectrum, gain_re, gain_im, basis_low, basis_rest)
    return (
        motion.reshape(tall, components, sites, NT),
        peaks.reshape(tall, components, sites, PERIODS),
    )


def solution(mesh):
    in_specs = (
        P("sub", None, None, None, "site", None),
        P("sub", None),
        P("sub", None, None, None),
        P(),
        P(),
    )
    out_specs = (P("sub", None, "site", None), P("sub", None, "site", None))
    return jax.shard_map(
        per_device, mesh=mesh, in_specs=in_specs, out_specs=out_specs, check_vma=False
    )
```

```python
import functools
import math

import jax
import jax.numpy as jnp
from jax import lax
from jax.experimental import pallas as pl
from jax.experimental.pallas import tpu as pltpu
from jax.sharding import PartitionSpec as P

NT = 2048
PERIODS = 40

damping = 0.05
sample_step = 0.1

LANES = 128
STRAINS = 6
BLOCK = 4
GROUP = 16
BF16 = jnp.bfloat16
F32 = jnp.float32


def basis_angles(freq_count, sample_count, fine):
    freq_ids = jnp.arange(freq_count, dtype=jnp.int32)
    tables = []
    for time_ids in (jnp.arange(0, sample_count, fine), jnp.arange(fine)):
        angles = (time_ids.astype(jnp.int32)[:, None] * freq_ids[None, :] % sample_count).astype(
            F32
        ) * (2.0 * math.pi / sample_count)
        tables += [jnp.cos(angles), jnp.sin(angles)]
    return tables


def oscillator_gains(period_count, freq_count, sample_count):
    period_ids = jnp.arange(period_count, dtype=F32)
    periods = 2.0 * jnp.exp(period_ids * (math.log(5.0) / max(period_count - 1, 1)))
    natural = 2.0 * math.pi / periods
    omega_bins = jnp.arange(freq_count, dtype=F32) * (2.0 * math.pi / (sample_count * sample_step))
    squared_natural = (natural * natural)[:, None]
    real_part = squared_natural - (omega_bins * omega_bins)[None, :]
    imag_part = 2.0 * damping * natural[:, None] * omega_bins[None, :]
    magnitude = real_part * real_part + imag_part * imag_part
    return (-squared_natural * real_part / magnitude, squared_natural * imag_part / magnitude)


def swap_blocks(parts):
    count = len(parts)
    width = LANES // count
    parts = list(parts)
    group = lax.broadcasted_iota(jnp.int32, parts[0].shape, 1) // width
    step = 1
    while step < count:
        low_lanes = (group & step) == 0
        for x in range(count):
            if x & step:
                continue
            low, high = parts[x], parts[x | step]
            parts[x] = jnp.where(low_lanes, low, pltpu.roll(high, width * step, 1))
            parts[x | step] = jnp.where(low_lanes, pltpu.roll(low, LANES - width * step, 1), high)
        step *= 2
    return parts


def pack_slip_kernel(workers, slip_hbm, mech_ref, out_ref, narrow, wide, padded, done):
    core = lax.rem(lax.axis_index("site"), 2)
    stride = 2 * workers
    slots = mech_ref.shape[1]
    rows = out_ref.shape[1] - slots
    pieces = done.shape[0]
    height = rows // pieces
    copies = []
    for i in range(pieces):
        here = pl.ds(i * height * stride, height * stride)
        copies.append(pltpu.make_async_copy(slip_hbm.at[here, :], narrow.at[here, :], done.at[i]))
        copies[i].start()
    padded[...] = jnp.zeros_like(padded)
    padded[:STRAINS, :slots] = mech_ref[...]
    moments = padded[...].T[:slots, :]
    first = moments.astype(BF16).astype(F32)
    second = (moments - first).astype(BF16).astype(F32)
    third = moments - first - second
    coded = (
        first + pltpu.roll(second, STRAINS, 1) + pltpu.roll(third, 2 * STRAINS, 1)
    ).astype(BF16)
    for d in range(workers):
        out_ref[d, rows:, :] = coded
    chunk = 16
    for i in range(pieces):
        copies[i].wait()
        here = pl.ds(i * height * stride, height * stride)
        wide[here, :] = narrow[here, :].astype(F32)
        for start in range(i * height, (i + 1) * height, chunk):
            parts = [
                wide[pl.ds(start * stride + 2 * x + core, chunk, stride=stride), :]
                for x in range(workers)
            ]
            for d, part in enumerate(swap_blocks(parts)):
                out_ref[d, start : start + chunk, :] = part.astype(BF16)


def choose_kernel(point_ref, chosen_ref):
    points, total = chosen_ref.shape
    point_ids = lax.axis_index("sub") * points + lax.broadcasted_iota(
        jnp.int32, (points, total), 0
    )
    chosen_ref[...] = (point_ref[...] == point_ids).astype(F32).astype(BF16)


def project_kernel(workers, chosen_ref, recv_ref, sgt_ref, out_ref, moments, wide):
    points = sgt_ref.shape[0]
    sites = sgt_ref.shape[4]
    mech_start = recv_ref.shape[1] - chosen_ref.shape[1] // workers
    coded = jnp.concatenate([recv_ref[w, mech_start:, :] for w in range(workers)], axis=0)
    coded = jnp.dot(chosen_ref[...], coded, preferred_element_type=F32)
    moments[...] = (
        coded + pltpu.roll(coded, LANES - STRAINS, 1) + pltpu.roll(coded, LANES - 2 * STRAINS, 1)
    )
    height = 4 * sites

    def one_point(row):
        moment = moments[pl.ds(row, 1), :]
        weights = [
            jnp.broadcast_to(moment[:, m : m + 1], (sites, LANES)) for m in range(STRAINS)
        ]
        for p in range(2):
            for c in range(2):
                combined = weights[0] * sgt_ref[row, p, c, 0].astype(F32)
                for m in range(1, STRAINS):
                    combined = combined + weights[m] * sgt_ref[row, p, c, m].astype(F32)
                start = pl.multiple_of(row * height + (2 * p + c) * sites, sites)
                wide[pl.ds(start, sites), :] = combined.astype(BF16).astype(F32)

    group = 8

    def some_points(step, carry):
        for u in range(group):
            one_point(step * group + u)
        return carry

    lax.fori_loop(0, points // group, some_points, 0)
    rows = out_ref.shape[1]
    chunk = 16
    for start in range(0, rows, chunk):
        parts = [
            wide[pl.ds(start * workers + x, chunk, stride=workers), :] for x in range(workers)
        ]
        for d, part in enumerate(swap_blocks(parts)):
            out_ref[d, start : start + chunk, :] = part.astype(BF16)


def gather_kernel(
    workers,
    tall,
    high,
    point_ref,
    count_ref,
    own_ref,
    other_ref,
    start_ref,
    block_ref,
    spread_hbm,
    slip,
    line_ref,
    wide,
    spread_ref,
    done,
):
    core = lax.rem(lax.axis_index("site"), 2)
    total = point_ref.shape[0]
    slots = total // workers
    slip_rows = slots * tall
    height = workers * tall
    for w in range(workers):
        here = slice(w * slip_rows, (w + 1) * slip_rows)
        slip[core, here, :] = own_ref[w, :slip_rows, :].astype(F32)
        slip[1 - core, here, :] = other_ref[w, :slip_rows, :].astype(F32)

    def note_worker(w, filled):
        def note_slot(k, carry):
            j = w * slots + k
            start_ref[filled + k] = point_ref[j] * high
            line_ref[filled + k] = j * tall
            return carry

        count = count_ref[w]
        lax.fori_loop(0, count, note_slot, 0)
        return filled + count

    amount = lax.fori_loop(0, workers, note_worker, 0)
    blocks = (amount + 2 * BLOCK - 1) // (2 * BLOCK)
    for extra in range(GROUP):
        start_ref[amount + extra] = 0
        line_ref[amount + extra] = 0

    width = LANES // workers
    group = lax.broadcasted_iota(jnp.int32, (tall, LANES), 1) // width
    row_ids = lax.broadcasted_iota(jnp.int32, (LANES, LANES), 0)
    lane_ids = lax.broadcasted_iota(jnp.int32, (LANES, LANES), 1)
    repeat = (row_ids % width == lane_ids % width).astype(F32).astype(BF16)

    def spread_slots(step, carry):
        for i in range(GROUP):
            index = step * GROUP + i
            for p in range(2):
                packed = slip[p, pl.ds(pl.multiple_of(line_ref[index], tall), tall), :]
                for x in range(workers):
                    wide[i, p, x * tall : (x + 1) * tall, :] = jnp.where(
                        (group == x) & (index < amount), packed, 0.0
                    )
        for i in range(GROUP):
            start = pl.multiple_of((step * GROUP + i) * height, height)
            for p in range(2):
                spread_ref[p, pl.ds(start, height), :] = jnp.dot(
                    wide[i, p].astype(BF16), repeat, preferred_element_type=F32
                ).astype(BF16)
        return carry

    lax.fori_loop(0, (amount + GROUP - 1) // GROUP, spread_slots, 0)
    block_ref[0] = blocks
    copy = pltpu.make_async_copy(spread_ref, spread_hbm, done)
    copy.start()
    copy.wait()


def contract_kernel(
    workers, tall, start_ref, block_ref, spread_hbm, proj_ref, out_ref, proj, even, odd, total, ordered, spread_ref, done
):
    proj_rows = proj_ref.shape[1]
    high = ordered.shape[0] // (workers * tall)
    half = high // 2
    variations = workers * tall
    lines = min(2, half)
    early = 2 * 2 * BLOCK * variations
    copies = [
        pltpu.make_async_copy(spread_hbm.at[:, part, :], spread_ref.at[:, part, :], done.at[i])
        for i, part in enumerate((pl.ds(0, early), pl.ds(early, spread_ref.shape[1] - early)))
    ]
    for copy in copies:
        copy.start()
    for w in range(workers):
        proj[w * proj_rows : (w + 1) * proj_rows, :] = proj_ref[w].astype(F32)
    total[...] = jnp.zeros_like(total)

    def widen_block(first, spread):
        for i in range(BLOCK):
            here = pl.ds(pl.multiple_of((first + i) * variations, variations), variations)
            real = spread_ref[0, here, :].astype(F32)
            imag = spread_ref[1, here, :].astype(F32)
            spread[0, i] = real + imag
            spread[1, i] = imag
            spread[2, i] = real

    def add_block(first, spread):
        starts = [start_ref[first + i] for i in range(BLOCK)]
        for line in range(0, half, lines):
            green = []
            for i in range(BLOCK):
                for y in range(line, line + lines):
                    real = jnp.broadcast_to(proj[pl.ds(starts[i] + y, 1), :], (tall, LANES))
                    imag = jnp.broadcast_to(proj[pl.ds(starts[i] + half + y, 1), :], (tall, LANES))
                    green.append((real, real + imag, imag - real))
            for x in range(workers):
                sums = [
                    [total[kind, y, x] for kind in range(3)] for y in range(line, line + lines)
                ]
                for i in range(BLOCK):
                    factors = [spread[kind, i, x * tall : (x + 1) * tall, :] for kind in range(3)]
                    for y in range(lines):
                        for kind in range(3):
                            sums[y][kind] = (
                                sums[y][kind] + green[i * lines + y][kind] * factors[kind]
                            )
                for y in range(lines):
                    for kind in range(3):
                        total[kind, line + y, x] = sums[y][kind]

    def add_two_blocks(step, carry):
        first = step * (2 * BLOCK)
        widen_block(first, even)
        widen_block(first + BLOCK, odd)
        add_block(first, even)
        add_block(first + BLOCK, odd)
        return carry

    copies[0].wait()
    lax.fori_loop(0, jnp.minimum(2, block_ref[0]), add_two_blocks, 0)
    copies[1].wait()
    lax.fori_loop(2, block_ref[0], add_two_blocks, 0)
    for y in range(half):
        for x in range(workers):
            shared = total[0, y, x]
            at_real = (y * workers + x) * tall
            at_imag = ((half + y) * workers + x) * tall
            ordered[at_real : at_real + tall, :] = shared - total[1, y, x]
            ordered[at_imag : at_imag + tall, :] = shared + total[2, y, x]
    for d in range(workers):
        for v in range(tall):
            y, x = divmod(d * tall + v, workers)
            out_ref[d, v * high : (v + 1) * high, :] = ordered[
                pl.ds(x * tall + y, high, stride=variations), :
            ]


def dot_rows(a, b):
    return lax.dot_general(a, b, (((1,), (1,)), ((), ())), preferred_element_type=F32)


def tables_kernel(
    coarse_cos_ref, coarse_sin_ref, fine_cos_ref, fine_sin_ref, ready_hbm, basis_ref, rest_ref
):
    del ready_hbm
    fine, freqs = fine_cos_ref.shape
    norm_scale = 1.0 / math.sqrt(freqs)
    cosine = norm_scale * fine_cos_ref[...]
    sine = norm_scale * fine_sin_ref[...]
    for i in range(coarse_cos_ref.shape[0]):
        start_cos, start_sin = coarse_cos_ref[i : i + 1, :], coarse_sin_ref[i : i + 1, :]
        here = slice(i * fine, (i + 1) * fine)
        for part, values in enumerate(
            (start_cos * cosine - start_sin * sine, -(start_sin * cosine) - start_cos * sine)
        ):
            low = values.astype(BF16)
            basis_ref[here, part * freqs : (part + 1) * freqs] = low
            rest_ref[here, part * freqs : (part + 1) * freqs] = (
                values - low.astype(F32)
            ).astype(BF16)


def synthesis_kernel(
    workers,
    tall,
    recv_ref,
    gain_re_ref,
    gain_im_ref,
    basis_ref,
    rest_ref,
    motion_ref,
    peak_ref,
    natural,
    peaks,
):
    freqs = natural.shape[1]
    rows = recv_ref.shape[1]
    for x, part in enumerate(swap_blocks([recv_ref[w] for w in range(workers)])):
        natural[pl.ds(x, rows, stride=workers), :] = part
    width = natural.shape[0] // (2 * tall)
    real = jnp.concatenate(
        [natural[(2 * v) * width : (2 * v + 1) * width, :] for v in range(tall)], axis=0
    )
    imag = jnp.concatenate(
        [natural[(2 * v + 1) * width : (2 * v + 2) * width, :] for v in range(tall)], axis=0
    )
    real_main, imag_main = real.astype(BF16), imag.astype(BF16)
    main = jnp.concatenate([real_main, imag_main], axis=1)
    rest = jnp.concatenate(
        [
            (real - real_main.astype(F32)).astype(BF16),
            (imag - imag_main.astype(F32)).astype(BF16),
        ],
        axis=1,
    )
    samples = basis_ref.shape[0]
    tile = 256
    for t in range(0, samples, tile):
        motion = dot_rows(main, basis_ref[t : t + tile, :])
        motion = motion + dot_rows(rest, basis_ref[t : t + tile, :])
        motion = motion + dot_rows(main, rest_ref[t : t + tile, :])
        motion_ref[:, t : t + tile] = motion.astype(BF16)
    tile = 512

    def one_period(q):
        gain_re = gain_re_ref[pl.ds(q, 1), :]
        gain_im = gain_im_ref[pl.ds(q, 1), :]
        response = jnp.concatenate(
            [
                (gain_re * real - gain_im * imag).astype(BF16),
                (gain_re * imag + gain_im * real).astype(BF16),
            ],
            axis=1,
        )
        peak = None
        for t in range(0, samples, tile):
            wave = jnp.abs(dot_rows(basis_ref[t : t + tile, :], response))
            wave = jnp.max(wave.reshape(tile // 8, 8, wave.shape[1]), axis=0)
            peak = wave if peak is None else jnp.maximum(peak, wave)
        peaks[pl.ds(q, 1), :] = jnp.max(peak, axis=0, keepdims=True)

    periods = gain_re_ref.shape[0]
    group = 20

    def some_periods(i, carry):
        for u in range(group):
            one_period(i * group + u)
        return carry

    lax.fori_loop(0, periods // group, some_periods, 0)
    for q in range(periods - periods % group, periods):
        one_period(q)
    peak_ref[...] = peaks[...].T[:, :periods]


def vmem():
    return pl.BlockSpec(memory_space=pltpu.VMEM)


def hbm():
    return pl.BlockSpec(memory_space=pltpu.HBM)


def smem():
    return pl.BlockSpec(memory_space=pltpu.SMEM)


def params(mebibytes, held=0):
    return pltpu.CompilerParams(vmem_limit_bytes=mebibytes * 2**20 + held)


def beside(microseconds):
    return pl.CostEstimate(
        flops=microseconds * 10**9, bytes_accessed=microseconds * 3 * 10**6, transcendentals=0
    )


def per_device(sgt, mechanism, slip, point_list, subfault_counts):
    workers = lax.axis_size("sub")
    site_parts = lax.axis_size("site")
    slots, variations, _, freqs = slip.shape
    points, _, components, _, sites, _ = sgt.shape
    total = point_list.shape[0]
    tall = variations // workers
    high = 2 * components * sites // workers
    slip_rows = slots * tall
    proj_rows = points * high
    flat = slip.reshape(slots * variations * 2, freqs)
    packed = pl.pallas_call(
        functools.partial(pack_slip_kernel, workers),
        out_shape=jax.ShapeDtypeStruct((workers, slip_rows + slots, LANES), BF16),
        in_specs=[hbm(), vmem()],
        out_specs=vmem(),
        scratch_shapes=[
            pltpu.VMEM(flat.shape, BF16),
            pltpu.VMEM(flat.shape, F32),
            pltpu.VMEM((LANES, LANES), F32),
            pltpu.SemaphoreType.DMA((4,)),
        ],
        compiler_params=params(58),
        name="pack_slip",
    )(flat, mechanism.T)
    own = lax.all_to_all(packed, "sub", split_axis=0, concat_axis=0, tiled=True)
    other = lax.ppermute(own, "site", [(i, i ^ 1) for i in range(site_parts)])
    chosen = pl.pallas_call(
        choose_kernel,
        out_shape=jax.ShapeDtypeStruct((points, total), BF16),
        in_specs=[vmem()],
        out_specs=vmem(),
        cost_estimate=beside(10),
        name="choose",
    )(point_list.reshape(1, total))
    projected = pl.pallas_call(
        functools.partial(project_kernel, workers),
        out_shape=jax.ShapeDtypeStruct((workers, proj_rows, LANES), BF16),
        in_specs=[vmem(), vmem(), vmem()],
        out_specs=vmem(),
        scratch_shapes=[
            pltpu.VMEM((points, LANES), F32),
            pltpu.VMEM((proj_rows * workers, LANES), F32),
        ],
        compiler_params=params(24),
        name="project",
    )(chosen, own, sgt)
    chunks = lax.all_to_all(projected, "sub", split_axis=0, concat_axis=0, tiled=True)
    capacity = total // 2 + GROUP
    spread_bytes = 2 * capacity * variations * LANES * 2
    starts, blocks, spread = pl.pallas_call(
        functools.partial(gather_kernel, workers, tall, high),
        out_shape=(
            jax.ShapeDtypeStruct((total + GROUP,), jnp.int32),
            jax.ShapeDtypeStruct((1,), jnp.int32),
            jax.ShapeDtypeStruct((2, capacity * variations, LANES), BF16),
        ),
        in_specs=[smem(), smem(), vmem(), vmem()],
        out_specs=(smem(), smem(), hbm()),
        scratch_shapes=[
            pltpu.VMEM((2, workers * slip_rows, LANES), F32),
            pltpu.SMEM((total + GROUP,), jnp.int32),
            pltpu.VMEM((GROUP, 2, variations, LANES), F32),
            pltpu.VMEM((2, capacity * variations, LANES), BF16),
            pltpu.SemaphoreType.DMA,
        ],
        compiler_params=params(16, spread_bytes),
        name="gather",
    )(point_list, subfault_counts, own, other)
    partial_rows = tall * high
    spectrum = pl.pallas_call(
        functools.partial(contract_kernel, workers, tall),
        out_shape=jax.ShapeDtypeStruct((workers, partial_rows, LANES), F32),
        in_specs=[smem(), smem(), hbm(), vmem()],
        out_specs=vmem(),
        scratch_shapes=[
            pltpu.VMEM((workers * proj_rows, LANES), F32),
            pltpu.VMEM((3, BLOCK, variations, LANES), F32),
            pltpu.VMEM((3, BLOCK, variations, LANES), F32),
            pltpu.VMEM((3, high // 2, workers, tall, LANES), F32),
            pltpu.VMEM((high * variations, LANES), F32),
            pltpu.VMEM((2, capacity * variations, LANES), BF16),
            pltpu.SemaphoreType.DMA((2,)),
        ],
        compiler_params=params(12, spread_bytes),
        name="contract",
    )(starts, blocks, spread, chunks)
    basis, basis_rest = pl.pallas_call(
        tables_kernel,
        out_shape=(jax.ShapeDtypeStruct((NT, 2 * freqs), BF16),) * 2,
        in_specs=[vmem()] * 4 + [hbm()],
        out_specs=(vmem(), vmem()),
        compiler_params=params(16),
        name="tables",
    )(*basis_angles(freqs, NT, 64), spectrum)
    gains = oscillator_gains(PERIODS, freqs, NT)
    spectrum = lax.all_to_all(spectrum, "sub", split_axis=0, concat_axis=0, tiled=True)
    width = tall * components * sites
    motion, peaks = pl.pallas_call(
        functools.partial(synthesis_kernel, workers, tall),
        out_shape=(
            jax.ShapeDtypeStruct((width, NT), BF16),
            jax.ShapeDtypeStruct((width, PERIODS), F32),
        ),
        in_specs=[vmem()] * 5,
        out_specs=(vmem(), vmem()),
        scratch_shapes=[
            pltpu.VMEM((2 * width, freqs), F32),
            pltpu.VMEM((LANES, width), F32),
        ],
        compiler_params=params(32),
        name="synthesis",
    )(spectrum, *gains, basis, basis_rest)
    return (
        motion.reshape(tall, components, sites, NT),
        peaks.reshape(tall, components, sites, PERIODS),
    )


def solution(mesh):
    in_specs = (
        P("sub", None, None, None, "site", None),
        P("sub", None),
        P("sub", None, None, None),
        P(),
        P(),
    )
    out_specs = (P("sub", None, "site", None), P("sub", None, "site", None))
    return jax.shard_map(
        per_device, mesh=mesh, in_specs=in_specs, out_specs=out_specs, check_vma=False
    )
```

```python
import functools
import math

import jax
import jax.numpy as jnp
from jax import lax
from jax.experimental import pallas as pl
from jax.experimental.pallas import tpu as pltpu
from jax.sharding import PartitionSpec as P

NT = 2048
PERIODS = 40

damping = 0.05
sample_step = 0.1

LANES = 128
STRAINS = 6
BLOCK = 4
GROUP = 16
BF16 = jnp.bfloat16
F32 = jnp.float32


def basis_angles(freq_count, sample_count, fine):
    freq_ids = jnp.arange(freq_count, dtype=jnp.int32)
    tables = []
    for time_ids in (jnp.arange(0, sample_count, fine), jnp.arange(fine)):
        angles = (time_ids.astype(jnp.int32)[:, None] * freq_ids[None, :] % sample_count).astype(
            F32
        ) * (2.0 * math.pi / sample_count)
        tables += [jnp.cos(angles), jnp.sin(angles)]
    return tables


def oscillator_gains(period_count, freq_count, sample_count):
    period_ids = jnp.arange(period_count, dtype=F32)
    periods = 2.0 * jnp.exp(period_ids * (math.log(5.0) / max(period_count - 1, 1)))
    natural = 2.0 * math.pi / periods
    omega_bins = jnp.arange(freq_count, dtype=F32) * (2.0 * math.pi / (sample_count * sample_step))
    squared_natural = (natural * natural)[:, None]
    real_part = squared_natural - (omega_bins * omega_bins)[None, :]
    imag_part = 2.0 * damping * natural[:, None] * omega_bins[None, :]
    magnitude = real_part * real_part + imag_part * imag_part
    return (-squared_natural * real_part / magnitude, squared_natural * imag_part / magnitude)


def swap_blocks(parts):
    count = len(parts)
    width = LANES // count
    parts = list(parts)
    group = lax.broadcasted_iota(jnp.int32, parts[0].shape, 1) // width
    step = 1
    while step < count:
        low_lanes = (group & step) == 0
        for x in range(count):
            if x & step:
                continue
            low, high = parts[x], parts[x | step]
            parts[x] = jnp.where(low_lanes, low, pltpu.roll(high, width * step, 1))
            parts[x | step] = jnp.where(low_lanes, pltpu.roll(low, LANES - width * step, 1), high)
        step *= 2
    return parts


def pack_slip_kernel(workers, slip_hbm, mech_hbm, out_hbm, narrow, mech_ref, out_ref, wide, padded, done, mech_done, sent):
    core = lax.rem(lax.axis_index("site"), 2)
    stride = 2 * workers
    slots = mech_ref.shape[1]
    rows = out_ref.shape[1] - slots
    pieces = done.shape[0]
    height = rows // pieces
    copies = []
    for i in range(pieces):
        here = pl.ds(i * height * stride, height * stride)
        copies.append(pltpu.make_async_copy(slip_hbm.at[here, :], narrow.at[here, :], done.at[i]))
        copies[i].start()
    mech_copy = pltpu.make_async_copy(mech_hbm, mech_ref, mech_done)
    mech_copy.start()
    padded[...] = jnp.zeros_like(padded)
    mech_copy.wait()
    padded[:STRAINS, :slots] = mech_ref[...]
    moments = padded[...].T[:slots, :]
    first = moments.astype(BF16).astype(F32)
    second = (moments - first).astype(BF16).astype(F32)
    third = moments - first - second
    coded = (
        first + pltpu.roll(second, STRAINS, 1) + pltpu.roll(third, 2 * STRAINS, 1)
    ).astype(BF16)
    for d in range(workers):
        out_ref[d, rows:, :] = coded
    sends = [
        pltpu.make_async_copy(out_ref.at[:, part, :], out_hbm.at[:, part, :], sent.at[i])
        for i, part in enumerate(
            [pl.ds(i * height, height) for i in range(pieces)] + [pl.ds(rows, slots)]
        )
    ]
    sends[pieces].start()
    chunk = 16
    for i in range(pieces):
        copies[i].wait()
        here = pl.ds(i * height * stride, height * stride)
        wide[here, :] = narrow[here, :].astype(F32)
        for start in range(i * height, (i + 1) * height, chunk):
            parts = [
                wide[pl.ds(start * stride + 2 * x + core, chunk, stride=stride), :]
                for x in range(workers)
            ]
            for d, part in enumerate(swap_blocks(parts)):
                out_ref[d, start : start + chunk, :] = part.astype(BF16)
        sends[i].start()
    for send in sends:
        send.wait()


def choose_kernel(point_ref, chosen_ref):
    points, total = chosen_ref.shape
    point_ids = lax.axis_index("sub") * points + lax.broadcasted_iota(
        jnp.int32, (points, total), 0
    )
    chosen_ref[...] = (point_ref[...] == point_ids).astype(F32)


def project_kernel(workers, chosen_ref, recv_ref, sgt_ref, out_ref, moments, wide):
    points = sgt_ref.shape[0]
    sites = sgt_ref.shape[4]
    mech_start = recv_ref.shape[1] - chosen_ref.shape[1] // workers
    coded = jnp.concatenate([recv_ref[w, mech_start:, :] for w in range(workers)], axis=0)
    coded = jnp.dot(chosen_ref[...], coded, preferred_element_type=F32)
    moments[...] = (
        coded + pltpu.roll(coded, LANES - STRAINS, 1) + pltpu.roll(coded, LANES - 2 * STRAINS, 1)
    )
    height = 4 * sites

    def one_point(row):
        moment = moments[pl.ds(row, 1), :]
        weights = [
            jnp.broadcast_to(moment[:, m : m + 1], (sites, LANES)) for m in range(STRAINS)
        ]
        for p in range(2):
            for c in range(2):
                combined = weights[0] * sgt_ref[row, p, c, 0].astype(F32)
                for m in range(1, STRAINS):
                    combined = combined + weights[m] * sgt_ref[row, p, c, m].astype(F32)
                start = pl.multiple_of(row * height + (2 * p + c) * sites, sites)
                wide[pl.ds(start, sites), :] = combined.astype(BF16).astype(F32)

    group = 8

    def some_points(step, carry):
        for u in range(group):
            one_point(step * group + u)
        return carry

    lax.fori_loop(0, points // group, some_points, 0)
    rows = out_ref.shape[1]
    chunk = 16
    for start in range(0, rows, chunk):
        parts = [
            wide[pl.ds(start * workers + x, chunk, stride=workers), :] for x in range(workers)
        ]
        for d, part in enumerate(swap_blocks(parts)):
            out_ref[d, start : start + chunk, :] = part.astype(BF16)


def gather_kernel(
    workers,
    tall,
    high,
    point_ref,
    count_ref,
    own_ref,
    other_ref,
    start_ref,
    block_ref,
    spread_hbm,
    slip,
    line_ref,
    wide,
    spread_ref,
    done,
):
    core = lax.rem(lax.axis_index("site"), 2)
    total = point_ref.shape[0]
    slots = total // workers
    slip_rows = slots * tall
    height = workers * tall
    for w in range(workers):
        here = slice(w * slip_rows, (w + 1) * slip_rows)
        slip[core, here, :] = own_ref[w, :slip_rows, :].astype(F32)
        slip[1 - core, here, :] = other_ref[w, :slip_rows, :].astype(F32)

    def note_worker(w, filled):
        def note_slot(k, carry):
            j = w * slots + k
            start_ref[filled + k] = point_ref[j] * high
            line_ref[filled + k] = j * tall
            return carry

        count = count_ref[w]
        lax.fori_loop(0, count, note_slot, 0)
        return filled + count

    amount = lax.fori_loop(0, workers, note_worker, 0)
    blocks = (amount + 2 * BLOCK - 1) // (2 * BLOCK)
    for extra in range(GROUP):
        start_ref[amount + extra] = 0
        line_ref[amount + extra] = 0

    width = LANES // workers
    group = lax.broadcasted_iota(jnp.int32, (tall, LANES), 1) // width
    row_ids = lax.broadcasted_iota(jnp.int32, (LANES, LANES), 0)
    lane_ids = lax.broadcasted_iota(jnp.int32, (LANES, LANES), 1)
    repeat = (row_ids % width == lane_ids % width).astype(F32).astype(BF16)

    def spread_slots(step, carry):
        for i in range(GROUP):
            index = step * GROUP + i
            for p in range(2):
                packed = slip[p, pl.ds(pl.multiple_of(line_ref[index], tall), tall), :]
                for x in range(workers):
                    wide[i, p, x * tall : (x + 1) * tall, :] = jnp.where(
                        (group == x) & (index < amount), packed, 0.0
                    )
        for i in range(GROUP):
            start = pl.multiple_of((step * GROUP + i) * height, height)
            for p in range(2):
                spread_ref[p, pl.ds(start, height), :] = jnp.dot(
                    wide[i, p].astype(BF16), repeat, preferred_element_type=F32
                ).astype(BF16)
        return carry

    lax.fori_loop(0, (amount + GROUP - 1) // GROUP, spread_slots, 0)
    block_ref[0] = blocks
    copy = pltpu.make_async_copy(spread_ref, spread_hbm, done)
    copy.start()
    copy.wait()


def contract_kernel(
    workers, tall, start_ref, block_ref, spread_ref, proj_ref, out_ref, proj, even, odd, total, ordered, outgoing
):
    proj_rows = proj_ref.shape[1]
    high = ordered.shape[0] // (workers * tall)
    half = high // 2
    variations = workers * tall
    lines = min(2, half)
    for w in range(workers):
        proj[w * proj_rows : (w + 1) * proj_rows, :] = proj_ref[w].astype(F32)
    total[...] = jnp.zeros_like(total)

    def widen_block(first, spread):
        for i in range(BLOCK):
            here = pl.ds(pl.multiple_of((first + i) * variations, variations), variations)
            real = spread_ref[0, here, :].astype(F32)
            imag = spread_ref[1, here, :].astype(F32)
            spread[0, i] = real + imag
            spread[1, i] = imag
            spread[2, i] = real

    def add_block(first, spread):
        starts = [start_ref[first + i] for i in range(BLOCK)]
        for line in range(0, half, lines):
            green = []
            for i in range(BLOCK):
                for y in range(line, line + lines):
                    real = jnp.broadcast_to(proj[pl.ds(starts[i] + y, 1), :], (tall, LANES))
                    imag = jnp.broadcast_to(proj[pl.ds(starts[i] + half + y, 1), :], (tall, LANES))
                    green.append((real, real + imag, imag - real))
            for x in range(workers):
                sums = [
                    [total[kind, y, x] for kind in range(3)] for y in range(line, line + lines)
                ]
                for i in range(BLOCK):
                    factors = [spread[kind, i, x * tall : (x + 1) * tall, :] for kind in range(3)]
                    for y in range(lines):
                        for kind in range(3):
                            sums[y][kind] = (
                                sums[y][kind] + green[i * lines + y][kind] * factors[kind]
                            )
                for y in range(lines):
                    for kind in range(3):
                        total[kind, line + y, x] = sums[y][kind]

    def add_two_blocks(step, carry):
        first = step * (2 * BLOCK)
        widen_block(first, even)
        widen_block(first + BLOCK, odd)
        add_block(first, even)
        add_block(first + BLOCK, odd)
        return carry

    lax.fori_loop(0, block_ref[0], add_two_blocks, 0)
    for y in range(half):
        for x in range(workers):
            shared = total[0, y, x]
            at_real = (y * workers + x) * tall
            at_imag = ((half + y) * workers + x) * tall
            ordered[at_real : at_real + tall, :] = shared - total[1, y, x]
            ordered[at_imag : at_imag + tall, :] = shared + total[2, y, x]
    for d in range(workers):
        for v in range(tall):
            y, x = divmod(d * tall + v, workers)
            outgoing[(d * tall + v) * high : (d * tall + v + 1) * high, :] = ordered[
                pl.ds(x * tall + y, high, stride=variations), :
            ]
    out_ref[...] = outgoing[...].astype(BF16)


def dot_rows(a, b):
    return lax.dot_general(a, b, (((1,), (1,)), ((), ())), preferred_element_type=F32)


def tables_kernel(
    coarse_cos_ref, coarse_sin_ref, fine_cos_ref, fine_sin_ref, ready_hbm, basis_ref, rest_ref
):
    del ready_hbm
    fine, freqs = fine_cos_ref.shape
    norm_scale = 1.0 / math.sqrt(freqs)
    cosine = norm_scale * fine_cos_ref[...]
    sine = norm_scale * fine_sin_ref[...]
    for i in range(coarse_cos_ref.shape[0]):
        start_cos, start_sin = coarse_cos_ref[i : i + 1, :], coarse_sin_ref[i : i + 1, :]
        here = slice(i * fine, (i + 1) * fine)
        for part, values in enumerate(
            (start_cos * cosine - start_sin * sine, -(start_sin * cosine) - start_cos * sine)
        ):
            low = values.astype(BF16)
            basis_ref[here, part * freqs : (part + 1) * freqs] = low
            rest_ref[here, part * freqs : (part + 1) * freqs] = (
                values - low.astype(F32)
            ).astype(BF16)


def synthesis_kernel(
    workers,
    tall,
    recv_ref,
    gain_re_ref,
    gain_im_ref,
    basis_ref,
    rest_ref,
    motion_hbm,
    peak_ref,
    received,
    natural,
    peaks,
    motion_ref,
    done,
):
    freqs = natural.shape[1]
    rows = recv_ref.shape[0] // workers
    received[...] = recv_ref[...].astype(F32)
    for x, part in enumerate(
        swap_blocks([received[w * rows : (w + 1) * rows, :] for w in range(workers)])
    ):
        natural[pl.ds(x, rows, stride=workers), :] = part
    width = natural.shape[0] // (2 * tall)
    real = jnp.concatenate(
        [natural[(2 * v) * width : (2 * v + 1) * width, :] for v in range(tall)], axis=0
    )
    imag = jnp.concatenate(
        [natural[(2 * v + 1) * width : (2 * v + 2) * width, :] for v in range(tall)], axis=0
    )
    spectrum = jnp.concatenate([real.astype(BF16), imag.astype(BF16)], axis=1)
    samples = basis_ref.shape[0]
    tile = samples // 4
    copies = []
    for i in range(4):
        here = slice(i * tile, (i + 1) * tile)
        motion = dot_rows(spectrum, basis_ref[here, :]) + dot_rows(spectrum, rest_ref[here, :])
        motion_ref[:, here] = motion.astype(BF16)
        copies.append(
            pltpu.make_async_copy(motion_ref.at[:, here], motion_hbm.at[:, here], done.at[i])
        )
        copies[i].start()

    def response_of(q):
        gain_re = gain_re_ref[q : q + 1, :]
        gain_im = gain_im_ref[q : q + 1, :]
        return jnp.concatenate(
            [
                (gain_re * real - gain_im * imag).astype(BF16),
                (gain_re * imag + gain_im * real).astype(BF16),
            ],
            axis=1,
        )

    def some_periods(first, number):
        response = jnp.concatenate([response_of(first + i) for i in range(number)], axis=0)
        peak = None
        for t in range(0, samples, tile):
            wave = jnp.abs(dot_rows(basis_ref[t : t + tile, :], response))
            wave = jnp.max(wave.reshape(tile // 8, 8, wave.shape[1]), axis=0)
            peak = wave if peak is None else jnp.maximum(peak, wave)
        top = jnp.max(peak, axis=0, keepdims=True)
        columns = top.shape[1] // number
        for i in range(number):
            peaks[first + i : first + i + 1, :] = top[:, i * columns : (i + 1) * columns]

    periods = gain_re_ref.shape[0]
    together = 2
    for first in range(0, periods, together):
        some_periods(first, min(together, periods - first))
    peak_ref[...] = peaks[...].T[:, :periods]
    for copy in copies:
        copy.wait()


def vmem():
    return pl.BlockSpec(memory_space=pltpu.VMEM)


def hbm():
    return pl.BlockSpec(memory_space=pltpu.HBM)


def smem():
    return pl.BlockSpec(memory_space=pltpu.SMEM)


def params(mebibytes, held=0):
    return pltpu.CompilerParams(vmem_limit_bytes=mebibytes * 2**20 + held)


def beside(microseconds):
    return pl.CostEstimate(
        flops=microseconds * 10**9, bytes_accessed=microseconds * 3 * 10**6, transcendentals=0
    )


def per_device(sgt, mechanism, slip, point_list, subfault_counts):
    workers = lax.axis_size("sub")
    site_parts = lax.axis_size("site")
    slots, variations, _, freqs = slip.shape
    points, _, components, _, sites, _ = sgt.shape
    total = point_list.shape[0]
    tall = variations // workers
    high = 2 * components * sites // workers
    slip_rows = slots * tall
    proj_rows = points * high
    flat = slip.reshape(slots * variations * 2, freqs)
    packed = pl.pallas_call(
        functools.partial(pack_slip_kernel, workers),
        out_shape=jax.ShapeDtypeStruct((workers, slip_rows + slots, LANES), BF16),
        in_specs=[hbm(), hbm()],
        out_specs=hbm(),
        scratch_shapes=[
            pltpu.VMEM(flat.shape, BF16),
            pltpu.VMEM((STRAINS, slots), F32),
            pltpu.VMEM((workers, slip_rows + slots, LANES), BF16),
            pltpu.VMEM(flat.shape, F32),
            pltpu.VMEM((LANES, LANES), F32),
            pltpu.SemaphoreType.DMA((4,)),
            pltpu.SemaphoreType.DMA,
            pltpu.SemaphoreType.DMA((5,)),
        ],
        compiler_params=params(58),
        name="pack_slip",
    )(flat, mechanism.T)
    own = lax.all_to_all(packed, "sub", split_axis=0, concat_axis=0, tiled=True)
    other = lax.ppermute(own, "site", [(i, i ^ 1) for i in range(site_parts)])
    chosen = pl.pallas_call(
        choose_kernel,
        out_shape=jax.ShapeDtypeStruct((points, total), F32),
        in_specs=[vmem()],
        out_specs=vmem(),
        cost_estimate=beside(10),
        name="choose",
    )(point_list.reshape(1, total)).astype(BF16)
    projected = pl.pallas_call(
        functools.partial(project_kernel, workers),
        out_shape=jax.ShapeDtypeStruct((workers, proj_rows, LANES), BF16),
        in_specs=[vmem(), vmem(), vmem()],
        out_specs=vmem(),
        scratch_shapes=[
            pltpu.VMEM((points, LANES), F32),
            pltpu.VMEM((proj_rows * workers, LANES), F32),
        ],
        compiler_params=params(24),
        name="project",
    )(chosen, own, sgt)
    chunks = lax.all_to_all(projected, "sub", split_axis=0, concat_axis=0, tiled=True)
    capacity = total // 2 + GROUP
    spread_bytes = 2 * capacity * variations * LANES * 2
    starts, blocks, spread = pl.pallas_call(
        functools.partial(gather_kernel, workers, tall, high),
        out_shape=(
            jax.ShapeDtypeStruct((total + GROUP,), jnp.int32),
            jax.ShapeDtypeStruct((1,), jnp.int32),
            jax.ShapeDtypeStruct((2, capacity * variations, LANES), BF16),
        ),
        in_specs=[smem(), smem(), vmem(), vmem()],
        out_specs=(smem(), smem(), hbm()),
        scratch_shapes=[
            pltpu.VMEM((2, workers * slip_rows, LANES), F32),
            pltpu.SMEM((total + GROUP,), jnp.int32),
            pltpu.VMEM((GROUP, 2, variations, LANES), F32),
            pltpu.VMEM((2, capacity * variations, LANES), BF16),
            pltpu.SemaphoreType.DMA,
        ],
        compiler_params=params(16, spread_bytes),
        name="gather",
    )(point_list, subfault_counts, own, other)
    partial_rows = tall * high
    spectrum = pl.pallas_call(
        functools.partial(contract_kernel, workers, tall),
        out_shape=jax.ShapeDtypeStruct((workers * partial_rows, LANES), BF16),
        in_specs=[smem(), smem(), vmem(), vmem()],
        out_specs=vmem(),
        scratch_shapes=[
            pltpu.VMEM((workers * proj_rows, LANES), F32),
            pltpu.VMEM((3, BLOCK, variations, LANES), F32),
            pltpu.VMEM((3, BLOCK, variations, LANES), F32),
            pltpu.VMEM((3, high // 2, workers, tall, LANES), F32),
            pltpu.VMEM((high * variations, LANES), F32),
            pltpu.VMEM((high * variations, LANES), F32),
        ],
        compiler_params=params(12, spread_bytes),
        name="contract",
    )(starts, blocks, spread, chunks)
    basis, basis_rest = pl.pallas_call(
        tables_kernel,
        out_shape=(jax.ShapeDtypeStruct((NT, 2 * freqs), BF16),) * 2,
        in_specs=[vmem()] * 4 + [hbm()],
        out_specs=(vmem(), vmem()),
        compiler_params=params(16),
        name="tables",
    )(*basis_angles(freqs, NT, 64), spectrum)
    gains = oscillator_gains(PERIODS, freqs, NT)
    spectrum = lax.all_to_all(spectrum, "sub", split_axis=0, concat_axis=0, tiled=True)
    width = tall * components * sites
    motion, peaks = pl.pallas_call(
        functools.partial(synthesis_kernel, workers, tall),
        out_shape=(
            jax.ShapeDtypeStruct((width, NT), BF16),
            jax.ShapeDtypeStruct((width, PERIODS), F32),
        ),
        in_specs=[vmem()] * 5,
        out_specs=(hbm(), vmem()),
        scratch_shapes=[
            pltpu.VMEM(spectrum.shape, F32),
            pltpu.VMEM((2 * width, freqs), F32),
            pltpu.VMEM((LANES, width), F32),
            pltpu.VMEM((width, NT), BF16),
            pltpu.SemaphoreType.DMA((4,)),
        ],
        compiler_params=params(32),
        name="synthesis",
    )(spectrum, *gains, basis, basis_rest)
    return (
        motion.reshape(tall, components, sites, NT),
        peaks.reshape(tall, components, sites, PERIODS),
    )


def solution(mesh):
    in_specs = (
        P("sub", None, None, None, "site", None),
        P("sub", None),
        P("sub", None, None, None),
        P(),
        P(),
    )
    out_specs = (P("sub", None, "site", None), P("sub", None, "site", None))
    return jax.shard_map(
        per_device, mesh=mesh, in_specs=in_specs, out_specs=out_specs, check_vma=False
    )
```

```python
import functools
import math

import jax
import jax.numpy as jnp
from jax import lax
from jax.experimental import pallas as pl
from jax.experimental.pallas import tpu as pltpu
from jax.sharding import PartitionSpec as P

NT = 2048
PERIODS = 40

damping = 0.05
sample_step = 0.1

LANES = 128
STRAINS = 6
BLOCK = 4
GROUP = 16
BF16 = jnp.bfloat16
F32 = jnp.float32


def basis_angles(freq_count, sample_count, fine):
    freq_ids = jnp.arange(freq_count, dtype=jnp.int32)
    tables = []
    for time_ids in (jnp.arange(0, sample_count, fine), jnp.arange(fine)):
        angles = (time_ids.astype(jnp.int32)[:, None] * freq_ids[None, :] % sample_count).astype(
            F32
        ) * (2.0 * math.pi / sample_count)
        tables += [jnp.cos(angles), jnp.sin(angles)]
    return tables


def oscillator_gains(period_count, freq_count, sample_count):
    period_ids = jnp.arange(period_count, dtype=F32)
    periods = 2.0 * jnp.exp(period_ids * (math.log(5.0) / max(period_count - 1, 1)))
    natural = 2.0 * math.pi / periods
    omega_bins = jnp.arange(freq_count, dtype=F32) * (2.0 * math.pi / (sample_count * sample_step))
    squared_natural = (natural * natural)[:, None]
    real_part = squared_natural - (omega_bins * omega_bins)[None, :]
    imag_part = 2.0 * damping * natural[:, None] * omega_bins[None, :]
    magnitude = real_part * real_part + imag_part * imag_part
    return (-squared_natural * real_part / magnitude, squared_natural * imag_part / magnitude)


def roll_groups(array, groups, count):
    shift = (groups % count) * (LANES // count)
    return pltpu.roll(array, shift, 1) if shift else array


def swap_blocks(parts):
    count = len(parts)
    group = lax.broadcasted_iota(jnp.int32, parts[0].shape, 1) // (LANES // count)
    step = 1
    while step < count:
        own = (group & step) == 0
        parts = [jnp.where(own, parts[i], parts[(i + step) % count]) for i in range(count)]
        step *= 2
    return [parts[-d % count] for d in range(count)]


def pack_slip_kernel(workers, slip_hbm, mech_hbm, out_hbm, narrow, mech_ref, out_ref, wide, padded, done, mech_done, sent):
    core = lax.rem(lax.axis_index("site"), 2)
    stride = 2 * workers
    slots = mech_ref.shape[1]
    rows = out_ref.shape[1] - slots
    pieces = done.shape[0]
    height = rows // pieces
    copies = []
    for i in range(pieces):
        here = pl.ds(i * height * stride, height * stride)
        copies.append(pltpu.make_async_copy(slip_hbm.at[here, :], narrow.at[here, :], done.at[i]))
        copies[i].start()
    mech_copy = pltpu.make_async_copy(mech_hbm, mech_ref, mech_done)
    mech_copy.start()
    padded[...] = jnp.zeros_like(padded)
    mech_copy.wait()
    padded[:STRAINS, :slots] = mech_ref[...]
    moments = padded[...].T[:slots, :]
    first = moments.astype(BF16).astype(F32)
    second = (moments - first).astype(BF16).astype(F32)
    third = moments - first - second
    coded = (
        first + pltpu.roll(second, STRAINS, 1) + pltpu.roll(third, 2 * STRAINS, 1)
    ).astype(BF16)
    for d in range(workers):
        out_ref[d, rows:, :] = coded
    sends = [
        pltpu.make_async_copy(out_ref.at[:, part, :], out_hbm.at[:, part, :], sent.at[i])
        for i, part in enumerate(
            [pl.ds(i * height, height) for i in range(pieces)] + [pl.ds(rows, slots)]
        )
    ]
    sends[pieces].start()
    chunk = 16
    for i in range(pieces):
        copies[i].wait()
        here = pl.ds(i * height * stride, height * stride)
        wide[here, :] = narrow[here, :].astype(F32)
        for start in range(i * height, (i + 1) * height, chunk):
            parts = [
                roll_groups(
                    wide[pl.ds(start * stride + 2 * x + core, chunk, stride=stride), :].astype(
                        BF16
                    ),
                    x,
                    workers,
                )
                for x in range(workers)
            ]
            for d, part in enumerate(swap_blocks(parts)):
                out_ref[d, start : start + chunk, :] = part
        sends[i].start()
    for send in sends:
        send.wait()


def choose_kernel(point_ref, chosen_ref):
    points, total = chosen_ref.shape
    point_ids = lax.axis_index("sub") * points + lax.broadcasted_iota(
        jnp.int32, (points, total), 0
    )
    chosen_ref[...] = (point_ref[...] == point_ids).astype(F32)


def project_kernel(workers, chosen_ref, recv_ref, sgt_ref, out_ref, moments, wide):
    points = sgt_ref.shape[0]
    sites = sgt_ref.shape[4]
    mech_start = recv_ref.shape[1] - chosen_ref.shape[1] // workers
    coded = jnp.concatenate([recv_ref[w, mech_start:, :] for w in range(workers)], axis=0)
    coded = jnp.dot(chosen_ref[...], coded, preferred_element_type=F32)
    moments[...] = (
        coded + pltpu.roll(coded, LANES - STRAINS, 1) + pltpu.roll(coded, LANES - 2 * STRAINS, 1)
    )
    height = 4 * sites

    def one_point(row):
        moment = moments[pl.ds(row, 1), :]
        weights = [
            jnp.broadcast_to(moment[:, m : m + 1], (sites, LANES)) for m in range(STRAINS)
        ]
        for p in range(2):
            for c in range(2):
                combined = weights[0] * sgt_ref[row, p, c, 0].astype(F32)
                for m in range(1, STRAINS):
                    combined = combined + weights[m] * sgt_ref[row, p, c, m].astype(F32)
                start = pl.multiple_of(row * height + (2 * p + c) * sites, sites)
                wide[pl.ds(start, sites), :] = combined.astype(BF16).astype(F32)

    group = 8

    def some_points(step, carry):
        for u in range(group):
            one_point(step * group + u)
        return carry

    lax.fori_loop(0, points // group, some_points, 0)
    rows = out_ref.shape[1]
    chunk = 16
    for start in range(0, rows, chunk):
        parts = [
            roll_groups(
                wide[pl.ds(start * workers + x, chunk, stride=workers), :].astype(BF16), x, workers
            )
            for x in range(workers)
        ]
        for d, part in enumerate(swap_blocks(parts)):
            out_ref[d, start : start + chunk, :] = part


def gather_kernel(
    workers,
    tall,
    high,
    point_ref,
    count_ref,
    own_ref,
    other_ref,
    start_ref,
    block_ref,
    spread_hbm,
    slip,
    line_ref,
    wide,
    spread_ref,
    done,
):
    core = lax.rem(lax.axis_index("site"), 2)
    total = point_ref.shape[0]
    slots = total // workers
    slip_rows = slots * tall
    height = workers * tall
    for w in range(workers):
        here = slice(w * slip_rows, (w + 1) * slip_rows)
        slip[core, here, :] = own_ref[w, :slip_rows, :].astype(F32)
        slip[1 - core, here, :] = other_ref[w, :slip_rows, :].astype(F32)

    def note_worker(w, filled):
        def note_slot(k, carry):
            j = w * slots + k
            start_ref[filled + k] = point_ref[j] * high
            line_ref[filled + k] = j * tall
            return carry

        count = count_ref[w]
        lax.fori_loop(0, count, note_slot, 0)
        return filled + count

    amount = lax.fori_loop(0, workers, note_worker, 0)
    blocks = (amount + 2 * BLOCK - 1) // (2 * BLOCK)
    for extra in range(GROUP):
        start_ref[amount + extra] = 0
        line_ref[amount + extra] = 0

    width = LANES // workers
    me = lax.axis_index("sub")
    group = lax.broadcasted_iota(jnp.int32, (tall, LANES), 1) // width
    row_ids = lax.broadcasted_iota(jnp.int32, (LANES, LANES), 0)
    lane_ids = lax.broadcasted_iota(jnp.int32, (LANES, LANES), 1)
    repeat = (row_ids % width == lane_ids % width).astype(F32).astype(BF16)

    def spread_slots(step, carry):
        for i in range(GROUP):
            index = step * GROUP + i
            for p in range(2):
                packed = slip[p, pl.ds(pl.multiple_of(line_ref[index], tall), tall), :]
                for x in range(workers):
                    wide[i, p, x * tall : (x + 1) * tall, :] = jnp.where(
                        (group == lax.rem(x + me, workers)) & (index < amount), packed, 0.0
                    )
        for i in range(GROUP):
            start = pl.multiple_of((step * GROUP + i) * height, height)
            for p in range(2):
                spread_ref[p, pl.ds(start, height), :] = jnp.dot(
                    wide[i, p].astype(BF16), repeat, preferred_element_type=F32
                ).astype(BF16)
        return carry

    lax.fori_loop(0, (amount + GROUP - 1) // GROUP, spread_slots, 0)
    block_ref[0] = blocks
    copy = pltpu.make_async_copy(spread_ref, spread_hbm, done)
    copy.start()
    copy.wait()


def contract_kernel(
    workers, tall, start_ref, block_ref, spread_ref, proj_ref, out_ref, proj, even, odd, total, ordered, outgoing
):
    proj_rows = proj_ref.shape[1]
    high = ordered.shape[0] // (workers * tall)
    half = high // 2
    variations = workers * tall
    lines = min(2, half)
    for w in range(workers):
        proj[w * proj_rows : (w + 1) * proj_rows, :] = proj_ref[w].astype(F32)
    total[...] = jnp.zeros_like(total)

    def widen_block(first, spread):
        for i in range(BLOCK):
            here = pl.ds(pl.multiple_of((first + i) * variations, variations), variations)
            real = spread_ref[0, here, :].astype(F32)
            imag = spread_ref[1, here, :].astype(F32)
            spread[0, i] = real + imag
            spread[1, i] = imag
            spread[2, i] = real

    def add_block(first, spread):
        starts = [start_ref[first + i] for i in range(BLOCK)]
        for line in range(0, half, lines):
            green = []
            for i in range(BLOCK):
                for y in range(line, line + lines):
                    real = jnp.broadcast_to(proj[pl.ds(starts[i] + y, 1), :], (tall, LANES))
                    imag = jnp.broadcast_to(proj[pl.ds(starts[i] + half + y, 1), :], (tall, LANES))
                    green.append((real, real + imag, imag - real))
            for x in range(workers):
                sums = [
                    [total[kind, y, x] for kind in range(3)] for y in range(line, line + lines)
                ]
                for i in range(BLOCK):
                    factors = [spread[kind, i, x * tall : (x + 1) * tall, :] for kind in range(3)]
                    for y in range(lines):
                        for kind in range(3):
                            sums[y][kind] = (
                                sums[y][kind] + green[i * lines + y][kind] * factors[kind]
                            )
                for y in range(lines):
                    for kind in range(3):
                        total[kind, line + y, x] = sums[y][kind]

    def add_two_blocks(step, carry):
        first = step * (2 * BLOCK)
        widen_block(first, even)
        widen_block(first + BLOCK, odd)
        add_block(first, even)
        add_block(first + BLOCK, odd)
        return carry

    lax.fori_loop(0, block_ref[0], add_two_blocks, 0)
    for y in range(half):
        for x in range(workers):
            shared = total[0, y, x]
            at_real = (y * workers + x) * tall
            at_imag = ((half + y) * workers + x) * tall
            ordered[at_real : at_real + tall, :] = shared - total[1, y, x]
            ordered[at_imag : at_imag + tall, :] = shared + total[2, y, x]
    for d in range(workers):
        for v in range(tall):
            y, x = divmod(d * tall + v, workers)
            outgoing[(d * tall + v) * high : (d * tall + v + 1) * high, :] = ordered[
                pl.ds(x * tall + y, high, stride=variations), :
            ]
    out_ref[...] = outgoing[...].astype(BF16)


def dot_rows(a, b):
    return lax.dot_general(a, b, (((1,), (1,)), ((), ())), preferred_element_type=F32)


def tables_kernel(
    coarse_cos_ref, coarse_sin_ref, fine_cos_ref, fine_sin_ref, ready_hbm, basis_ref, rest_ref
):
    del ready_hbm
    fine, freqs = fine_cos_ref.shape
    norm_scale = 1.0 / math.sqrt(freqs)
    cosine = norm_scale * fine_cos_ref[...]
    sine = norm_scale * fine_sin_ref[...]
    for i in range(coarse_cos_ref.shape[0]):
        start_cos, start_sin = coarse_cos_ref[i : i + 1, :], coarse_sin_ref[i : i + 1, :]
        here = slice(i * fine, (i + 1) * fine)
        for part, values in enumerate(
            (start_cos * cosine - start_sin * sine, -(start_sin * cosine) - start_cos * sine)
        ):
            low = values.astype(BF16)
            basis_ref[here, part * freqs : (part + 1) * freqs] = low
            rest_ref[here, part * freqs : (part + 1) * freqs] = (
                values - low.astype(F32)
            ).astype(BF16)


def synthesis_kernel(
    workers,
    tall,
    recv_ref,
    gain_re_ref,
    gain_im_ref,
    basis_ref,
    rest_ref,
    motion_hbm,
    peak_ref,
    received,
    natural,
    peaks,
    motion_ref,
    done,
):
    freqs = natural.shape[1]
    rows = recv_ref.shape[0] // workers
    if rows % 16:
        received[...] = recv_ref[...].astype(F32)
        parts = [received[w * rows : (w + 1) * rows, :] for w in range(workers)]
    else:
        parts = [recv_ref[w * rows : (w + 1) * rows, :] for w in range(workers)]
    for x, part in enumerate(swap_blocks(parts)):
        natural[pl.ds(x, rows, stride=workers), :] = roll_groups(part, -x, workers).astype(F32)
    width = natural.shape[0] // (2 * tall)
    real = jnp.concatenate(
        [natural[(2 * v) * width : (2 * v + 1) * width, :] for v in range(tall)], axis=0
    )
    imag = jnp.concatenate(
        [natural[(2 * v + 1) * width : (2 * v + 2) * width, :] for v in range(tall)], axis=0
    )
    spectrum = jnp.concatenate([real.astype(BF16), imag.astype(BF16)], axis=1)
    samples = basis_ref.shape[0]
    tile = samples // 4
    copies = []
    for i in range(4):
        here = slice(i * tile, (i + 1) * tile)
        motion = dot_rows(spectrum, basis_ref[here, :]) + dot_rows(spectrum, rest_ref[here, :])
        motion_ref[:, here] = motion.astype(BF16)
        copies.append(
            pltpu.make_async_copy(motion_ref.at[:, here], motion_hbm.at[:, here], done.at[i])
        )
        copies[i].start()

    def response_of(q):
        gain_re = gain_re_ref[q : q + 1, :]
        gain_im = gain_im_ref[q : q + 1, :]
        return jnp.concatenate(
            [
                (gain_re * real - gain_im * imag).astype(BF16),
                (gain_re * imag + gain_im * real).astype(BF16),
            ],
            axis=1,
        )

    def some_periods(first, number):
        response = jnp.concatenate([response_of(first + i) for i in range(number)], axis=0)
        peak = None
        for t in range(0, samples, tile):
            wave = jnp.abs(dot_rows(basis_ref[t : t + tile, :], response))
            wave = jnp.max(wave.reshape(tile // 8, 8, wave.shape[1]), axis=0)
            peak = wave if peak is None else jnp.maximum(peak, wave)
        top = jnp.max(peak, axis=0, keepdims=True)
        columns = top.shape[1] // number
        for i in range(number):
            peaks[first + i : first + i + 1, :] = top[:, i * columns : (i + 1) * columns]

    periods = gain_re_ref.shape[0]
    together = 2
    for first in range(0, periods, together):
        some_periods(first, min(together, periods - first))
    peak_ref[...] = peaks[...].T[:, :periods]
    for copy in copies:
        copy.wait()


def vmem():
    return pl.BlockSpec(memory_space=pltpu.VMEM)


def hbm():
    return pl.BlockSpec(memory_space=pltpu.HBM)


def smem():
    return pl.BlockSpec(memory_space=pltpu.SMEM)


def params(mebibytes, held=0):
    return pltpu.CompilerParams(vmem_limit_bytes=mebibytes * 2**20 + held)


def beside(microseconds):
    return pl.CostEstimate(
        flops=microseconds * 10**9, bytes_accessed=microseconds * 3 * 10**6, transcendentals=0
    )


def per_device(sgt, mechanism, slip, point_list, subfault_counts):
    workers = lax.axis_size("sub")
    site_parts = lax.axis_size("site")
    slots, variations, _, freqs = slip.shape
    points, _, components, _, sites, _ = sgt.shape
    total = point_list.shape[0]
    tall = variations // workers
    high = 2 * components * sites // workers
    slip_rows = slots * tall
    proj_rows = points * high
    flat = slip.reshape(slots * variations * 2, freqs)
    packed = pl.pallas_call(
        functools.partial(pack_slip_kernel, workers),
        out_shape=jax.ShapeDtypeStruct((workers, slip_rows + slots, LANES), BF16),
        in_specs=[hbm(), hbm()],
        out_specs=hbm(),
        scratch_shapes=[
            pltpu.VMEM(flat.shape, BF16),
            pltpu.VMEM((STRAINS, slots), F32),
            pltpu.VMEM((workers, slip_rows + slots, LANES), BF16),
            pltpu.VMEM(flat.shape, F32),
            pltpu.VMEM((LANES, LANES), F32),
            pltpu.SemaphoreType.DMA((4,)),
            pltpu.SemaphoreType.DMA,
            pltpu.SemaphoreType.DMA((5,)),
        ],
        compiler_params=params(58),
        name="pack_slip",
    )(flat, mechanism.T)
    own = lax.all_to_all(packed, "sub", split_axis=0, concat_axis=0, tiled=True)
    other = lax.ppermute(own, "site", [(i, i ^ 1) for i in range(site_parts)])
    chosen = pl.pallas_call(
        choose_kernel,
        out_shape=jax.ShapeDtypeStruct((points, total), F32),
        in_specs=[vmem()],
        out_specs=vmem(),
        cost_estimate=beside(10),
        name="choose",
    )(point_list.reshape(1, total)).astype(BF16)
    projected = pl.pallas_call(
        functools.partial(project_kernel, workers),
        out_shape=jax.ShapeDtypeStruct((workers, proj_rows, LANES), BF16),
        in_specs=[vmem(), vmem(), vmem()],
        out_specs=vmem(),
        scratch_shapes=[
            pltpu.VMEM((points, LANES), F32),
            pltpu.VMEM((proj_rows * workers, LANES), F32),
        ],
        compiler_params=params(24),
        name="project",
    )(chosen, own, sgt)
    chunks = lax.all_to_all(projected, "sub", split_axis=0, concat_axis=0, tiled=True)
    capacity = total // 2 + GROUP
    spread_bytes = 2 * capacity * variations * LANES * 2
    starts, blocks, spread = pl.pallas_call(
        functools.partial(gather_kernel, workers, tall, high),
        out_shape=(
            jax.ShapeDtypeStruct((total + GROUP,), jnp.int32),
            jax.ShapeDtypeStruct((1,), jnp.int32),
            jax.ShapeDtypeStruct((2, capacity * variations, LANES), BF16),
        ),
        in_specs=[smem(), smem(), vmem(), vmem()],
        out_specs=(smem(), smem(), hbm()),
        scratch_shapes=[
            pltpu.VMEM((2, workers * slip_rows, LANES), F32),
            pltpu.SMEM((total + GROUP,), jnp.int32),
            pltpu.VMEM((GROUP, 2, variations, LANES), F32),
            pltpu.VMEM((2, capacity * variations, LANES), BF16),
            pltpu.SemaphoreType.DMA,
        ],
        compiler_params=params(16, spread_bytes),
        name="gather",
    )(point_list, subfault_counts, own, other)
    partial_rows = tall * high
    spectrum = pl.pallas_call(
        functools.partial(contract_kernel, workers, tall),
        out_shape=jax.ShapeDtypeStruct((workers * partial_rows, LANES), BF16),
        in_specs=[smem(), smem(), vmem(), vmem()],
        out_specs=vmem(),
        scratch_shapes=[
            pltpu.VMEM((workers * proj_rows, LANES), F32),
            pltpu.VMEM((3, BLOCK, variations, LANES), F32),
            pltpu.VMEM((3, BLOCK, variations, LANES), F32),
            pltpu.VMEM((3, high // 2, workers, tall, LANES), F32),
            pltpu.VMEM((high * variations, LANES), F32),
            pltpu.VMEM((high * variations, LANES), F32),
        ],
        compiler_params=params(12, spread_bytes),
        name="contract",
    )(starts, blocks, spread, chunks)
    basis, basis_rest = pl.pallas_call(
        tables_kernel,
        out_shape=(jax.ShapeDtypeStruct((NT, 2 * freqs), BF16),) * 2,
        in_specs=[vmem()] * 4 + [hbm()],
        out_specs=(vmem(), vmem()),
        compiler_params=params(16),
        name="tables",
    )(*basis_angles(freqs, NT, 64), spectrum)
    gains = oscillator_gains(PERIODS, freqs, NT)
    spectrum = lax.all_to_all(spectrum, "sub", split_axis=0, concat_axis=0, tiled=True)
    width = tall * components * sites
    motion, peaks = pl.pallas_call(
        functools.partial(synthesis_kernel, workers, tall),
        out_shape=(
            jax.ShapeDtypeStruct((width, NT), BF16),
            jax.ShapeDtypeStruct((width, PERIODS), F32),
        ),
        in_specs=[vmem()] * 5,
        out_specs=(hbm(), vmem()),
        scratch_shapes=[
            pltpu.VMEM(spectrum.shape, F32),
            pltpu.VMEM((2 * width, freqs), F32),
            pltpu.VMEM((LANES, width), F32),
            pltpu.VMEM((width, NT), BF16),
            pltpu.SemaphoreType.DMA((4,)),
        ],
        compiler_params=params(32),
        name="synthesis",
    )(spectrum, *gains, basis, basis_rest)
    return (
        motion.reshape(tall, components, sites, NT),
        peaks.reshape(tall, components, sites, PERIODS),
    )


def solution(mesh):
    in_specs = (
        P("sub", None, None, None, "site", None),
        P("sub", None),
        P("sub", None, None, None),
        P(),
        P(),
    )
    out_specs = (P("sub", None, "site", None), P("sub", None, "site", None))
    return jax.shard_map(
        per_device, mesh=mesh, in_specs=in_specs, out_specs=out_specs, check_vma=False
    )
```

```python
import functools
import math

import jax
import jax.numpy as jnp
from jax import lax
from jax.experimental import pallas as pl
from jax.experimental.pallas import tpu as pltpu
from jax.sharding import PartitionSpec as P

NT = 2048
PERIODS = 40

damping = 0.05
sample_step = 0.1

LANES = 128
STRAINS = 6
BLOCK = 4
GROUP = 16
BF16 = jnp.bfloat16
F32 = jnp.float32


def basis_angles(freq_count, sample_count, fine):
    freq_ids = jnp.arange(freq_count, dtype=jnp.int32)
    tables = []
    for time_ids in (jnp.arange(0, sample_count, fine), jnp.arange(fine)):
        angles = (time_ids.astype(jnp.int32)[:, None] * freq_ids[None, :] % sample_count).astype(
            F32
        ) * (2.0 * math.pi / sample_count)
        tables += [jnp.cos(angles), jnp.sin(angles)]
    return tables


def oscillator_gains(period_count, freq_count, sample_count):
    period_ids = jnp.arange(period_count, dtype=F32)
    periods = 2.0 * jnp.exp(period_ids * (math.log(5.0) / max(period_count - 1, 1)))
    natural = 2.0 * math.pi / periods
    omega_bins = jnp.arange(freq_count, dtype=F32) * (2.0 * math.pi / (sample_count * sample_step))
    squared_natural = (natural * natural)[:, None]
    real_part = squared_natural - (omega_bins * omega_bins)[None, :]
    imag_part = 2.0 * damping * natural[:, None] * omega_bins[None, :]
    magnitude = real_part * real_part + imag_part * imag_part
    return (-squared_natural * real_part / magnitude, squared_natural * imag_part / magnitude)


def roll_groups(array, groups, count):
    shift = (groups % count) * (LANES // count)
    return pltpu.roll(array, shift, 1) if shift else array


def swap_blocks(parts):
    count = len(parts)
    group = lax.broadcasted_iota(jnp.int32, parts[0].shape, 1) // (LANES // count)
    step = 1
    while step < count:
        own = (group & step) == 0
        parts = [jnp.where(own, parts[i], parts[(i + step) % count]) for i in range(count)]
        step *= 2
    return [parts[-d % count] for d in range(count)]


def pack_slip_kernel(workers, slip_hbm, mech_hbm, out_hbm, narrow, mech_ref, out_ref, wide, padded, done, mech_done, sent):
    core = lax.rem(lax.axis_index("site"), 2)
    stride = 2 * workers
    slots = mech_ref.shape[1]
    rows = out_ref.shape[1] - slots
    pieces = done.shape[0]
    height = rows // pieces
    copies = []
    for i in range(pieces):
        here = pl.ds(i * height * stride, height * stride)
        copies.append(pltpu.make_async_copy(slip_hbm.at[here, :], narrow.at[here, :], done.at[i]))
        copies[i].start()
    mech_copy = pltpu.make_async_copy(mech_hbm, mech_ref, mech_done)
    mech_copy.start()
    padded[...] = jnp.zeros_like(padded)
    mech_copy.wait()
    padded[:STRAINS, :slots] = mech_ref[...]
    moments = padded[...].T[:slots, :]
    first = moments.astype(BF16).astype(F32)
    second = (moments - first).astype(BF16).astype(F32)
    third = moments - first - second
    coded = (
        first + pltpu.roll(second, STRAINS, 1) + pltpu.roll(third, 2 * STRAINS, 1)
    ).astype(BF16)
    for d in range(workers):
        out_ref[d, rows:, :] = coded
    sends = [
        pltpu.make_async_copy(out_ref.at[:, part, :], out_hbm.at[:, part, :], sent.at[i])
        for i, part in enumerate(
            [pl.ds(i * height, height) for i in range(pieces)] + [pl.ds(rows, slots)]
        )
    ]
    sends[pieces].start()
    chunk = 16
    for i in range(pieces):
        copies[i].wait()
        here = pl.ds(i * height * stride, height * stride)
        wide[here, :] = narrow[here, :].astype(F32)
        for start in range(i * height, (i + 1) * height, chunk):
            parts = [
                roll_groups(
                    wide[pl.ds(start * stride + 2 * x + core, chunk, stride=stride), :].astype(
                        BF16
                    ),
                    x,
                    workers,
                )
                for x in range(workers)
            ]
            for d, part in enumerate(swap_blocks(parts)):
                out_ref[d, start : start + chunk, :] = part
        sends[i].start()
    for send in sends:
        send.wait()


def choose_kernel(
    workers, tall, high, point_ref, slots_ref, count_ref, chosen_ref, start_ref, line_ref
):
    points, total = chosen_ref.shape
    slots = total // workers
    point_ids = lax.axis_index("sub") * points + lax.broadcasted_iota(
        jnp.int32, (points, total), 0
    )
    chosen_ref[...] = (point_ref[...] == point_ids).astype(F32)

    def note_worker(w, filled):
        def note_slot(k, carry):
            j = w * slots + k
            start_ref[filled + k] = slots_ref[j] * high
            line_ref[filled + k] = j * tall
            return carry

        count = count_ref[w]
        lax.fori_loop(0, count, note_slot, 0)
        return filled + count

    amount = lax.fori_loop(0, workers, note_worker, 0)
    for extra in range(GROUP):
        start_ref[amount + extra] = 0
        line_ref[amount + extra] = 0
    start_ref[total + GROUP] = (amount + 2 * BLOCK - 1) // (2 * BLOCK)
    line_ref[total + GROUP] = amount


def project_kernel(workers, chosen_ref, recv_ref, sgt_ref, out_ref, moments, wide):
    points = sgt_ref.shape[0]
    sites = sgt_ref.shape[4]
    mech_start = recv_ref.shape[1] - chosen_ref.shape[1] // workers
    coded = jnp.concatenate([recv_ref[w, mech_start:, :] for w in range(workers)], axis=0)
    coded = jnp.dot(chosen_ref[...], coded, preferred_element_type=F32)
    moments[...] = (
        coded + pltpu.roll(coded, LANES - STRAINS, 1) + pltpu.roll(coded, LANES - 2 * STRAINS, 1)
    )
    height = 4 * sites

    def one_point(row):
        moment = moments[pl.ds(row, 1), :]
        weights = [
            jnp.broadcast_to(moment[:, m : m + 1], (sites, LANES)) for m in range(STRAINS)
        ]
        for p in range(2):
            for c in range(2):
                combined = weights[0] * sgt_ref[row, p, c, 0].astype(F32)
                for m in range(1, STRAINS):
                    combined = combined + weights[m] * sgt_ref[row, p, c, m].astype(F32)
                start = pl.multiple_of(row * height + (2 * p + c) * sites, sites)
                wide[pl.ds(start, sites), :] = combined.astype(BF16).astype(F32)

    group = 8

    def some_points(step, carry):
        for u in range(group):
            one_point(step * group + u)
        return carry

    lax.fori_loop(0, points // group, some_points, 0)
    rows = out_ref.shape[1]
    chunk = 16
    for start in range(0, rows, chunk):
        parts = [
            roll_groups(
                wide[pl.ds(start * workers + x, chunk, stride=workers), :].astype(BF16), x, workers
            )
            for x in range(workers)
        ]
        for d, part in enumerate(swap_blocks(parts)):
            out_ref[d, start : start + chunk, :] = part


def gather_kernel(workers, tall, line_ref, own_ref, other_ref, spread_ref, slip, wide):
    core = lax.rem(lax.axis_index("site"), 2)
    total = line_ref.shape[0] - GROUP - 1
    amount = line_ref[total + GROUP]
    slip_rows = total // workers * tall
    height = workers * tall
    for w in range(workers):
        here = slice(w * slip_rows, (w + 1) * slip_rows)
        slip[core, here, :] = own_ref[w, :slip_rows, :].astype(F32)
        slip[1 - core, here, :] = other_ref[w, :slip_rows, :].astype(F32)
    width = LANES // workers
    me = lax.axis_index("sub")
    group = lax.broadcasted_iota(jnp.int32, (tall, LANES), 1) // width
    row_ids = lax.broadcasted_iota(jnp.int32, (LANES, LANES), 0)
    lane_ids = lax.broadcasted_iota(jnp.int32, (LANES, LANES), 1)
    repeat = (row_ids % width == lane_ids % width).astype(F32).astype(BF16)

    def spread_slots(step, carry):
        for i in range(GROUP):
            index = step * GROUP + i
            for p in range(2):
                packed = slip[p, pl.ds(pl.multiple_of(line_ref[index], tall), tall), :]
                for x in range(workers):
                    wide[i, p, x * tall : (x + 1) * tall, :] = jnp.where(
                        (group == lax.rem(x + me, workers)) & (index < amount), packed, 0.0
                    )
        for i in range(GROUP):
            start = pl.multiple_of((step * GROUP + i) * height, height)
            for p in range(2):
                spread_ref[p, pl.ds(start, height), :] = jnp.dot(
                    wide[i, p].astype(BF16), repeat, preferred_element_type=F32
                ).astype(BF16)
        return carry

    lax.fori_loop(0, (amount + GROUP - 1) // GROUP, spread_slots, 0)


def contract_kernel(
    workers, tall, start_ref, spread_ref, proj_ref, out_ref, proj, even, odd, total, ordered, outgoing
):
    proj_rows = proj_ref.shape[1]
    high = ordered.shape[0] // (workers * tall)
    half = high // 2
    variations = workers * tall
    lines = min(2, half)
    for w in range(workers):
        proj[w * proj_rows : (w + 1) * proj_rows, :] = proj_ref[w].astype(F32)
    total[...] = jnp.zeros_like(total)

    def widen_block(first, spread):
        for i in range(BLOCK):
            here = pl.ds(pl.multiple_of((first + i) * variations, variations), variations)
            real = spread_ref[0, here, :].astype(F32)
            imag = spread_ref[1, here, :].astype(F32)
            spread[0, i] = real + imag
            spread[1, i] = imag
            spread[2, i] = real

    def add_block(first, spread):
        starts = [start_ref[first + i] for i in range(BLOCK)]
        for line in range(0, half, lines):
            green = []
            for i in range(BLOCK):
                for y in range(line, line + lines):
                    real = jnp.broadcast_to(proj[pl.ds(starts[i] + y, 1), :], (tall, LANES))
                    imag = jnp.broadcast_to(proj[pl.ds(starts[i] + half + y, 1), :], (tall, LANES))
                    green.append((real, real + imag, imag - real))
            for x in range(workers):
                sums = [
                    [total[kind, y, x] for kind in range(3)] for y in range(line, line + lines)
                ]
                for i in range(BLOCK):
                    factors = [spread[kind, i, x * tall : (x + 1) * tall, :] for kind in range(3)]
                    for y in range(lines):
                        for kind in range(3):
                            sums[y][kind] = (
                                sums[y][kind] + green[i * lines + y][kind] * factors[kind]
                            )
                for y in range(lines):
                    for kind in range(3):
                        total[kind, line + y, x] = sums[y][kind]

    def add_two_blocks(step, carry):
        first = step * (2 * BLOCK)
        widen_block(first, even)
        widen_block(first + BLOCK, odd)
        add_block(first, even)
        add_block(first + BLOCK, odd)
        return carry

    lax.fori_loop(0, start_ref[start_ref.shape[0] - 1], add_two_blocks, 0)
    for y in range(half):
        for x in range(workers):
            shared = total[0, y, x]
            at_real = (y * workers + x) * tall
            at_imag = ((half + y) * workers + x) * tall
            ordered[at_real : at_real + tall, :] = shared - total[1, y, x]
            ordered[at_imag : at_imag + tall, :] = shared + total[2, y, x]
    for d in range(workers):
        for v in range(tall):
            y, x = divmod(d * tall + v, workers)
            outgoing[(d * tall + v) * high : (d * tall + v + 1) * high, :] = ordered[
                pl.ds(x * tall + y, high, stride=variations), :
            ]
    out_ref[...] = outgoing[...].astype(BF16)


def dot_rows(a, b):
    return lax.dot_general(a, b, (((1,), (1,)), ((), ())), preferred_element_type=F32)


def tables_kernel(
    coarse_cos_ref, coarse_sin_ref, fine_cos_ref, fine_sin_ref, ready_hbm, basis_ref, rest_ref
):
    del ready_hbm
    fine, freqs = fine_cos_ref.shape
    norm_scale = 1.0 / math.sqrt(freqs)
    cosine = norm_scale * fine_cos_ref[...]
    sine = norm_scale * fine_sin_ref[...]
    for i in range(coarse_cos_ref.shape[0]):
        start_cos, start_sin = coarse_cos_ref[i : i + 1, :], coarse_sin_ref[i : i + 1, :]
        here = slice(i * fine, (i + 1) * fine)
        for part, values in enumerate(
            (start_cos * cosine - start_sin * sine, -(start_sin * cosine) - start_cos * sine)
        ):
            low = values.astype(BF16)
            basis_ref[here, part * freqs : (part + 1) * freqs] = low
            rest_ref[here, part * freqs : (part + 1) * freqs] = (
                values - low.astype(F32)
            ).astype(BF16)


def synthesis_kernel(
    workers,
    tall,
    recv_ref,
    gain_re_ref,
    gain_im_ref,
    basis_ref,
    rest_ref,
    motion_hbm,
    peak_ref,
    received,
    natural,
    peaks,
    motion_ref,
    done,
):
    freqs = natural.shape[1]
    rows = recv_ref.shape[0] // workers
    if rows % 16:
        received[...] = recv_ref[...].astype(F32)
        parts = [received[w * rows : (w + 1) * rows, :] for w in range(workers)]
    else:
        parts = [recv_ref[w * rows : (w + 1) * rows, :] for w in range(workers)]
    for x, part in enumerate(swap_blocks(parts)):
        natural[pl.ds(x, rows, stride=workers), :] = roll_groups(part, -x, workers).astype(F32)
    width = natural.shape[0] // (2 * tall)
    real = jnp.concatenate(
        [natural[(2 * v) * width : (2 * v + 1) * width, :] for v in range(tall)], axis=0
    )
    imag = jnp.concatenate(
        [natural[(2 * v + 1) * width : (2 * v + 2) * width, :] for v in range(tall)], axis=0
    )
    spectrum = jnp.concatenate([real.astype(BF16), imag.astype(BF16)], axis=1)
    samples = basis_ref.shape[0]
    tile = samples // 4
    copies = []
    for i in range(4):
        here = slice(i * tile, (i + 1) * tile)
        motion = dot_rows(spectrum, basis_ref[here, :]) + dot_rows(spectrum, rest_ref[here, :])
        motion_ref[:, here] = motion.astype(BF16)
        copies.append(
            pltpu.make_async_copy(motion_ref.at[:, here], motion_hbm.at[:, here], done.at[i])
        )
        copies[i].start()

    def response_of(q):
        gain_re = gain_re_ref[q : q + 1, :]
        gain_im = gain_im_ref[q : q + 1, :]
        return jnp.concatenate(
            [
                (gain_re * real - gain_im * imag).astype(BF16),
                (gain_re * imag + gain_im * real).astype(BF16),
            ],
            axis=1,
        )

    def some_periods(first, number):
        response = jnp.concatenate([response_of(first + i) for i in range(number)], axis=0)
        peak = None
        for t in range(0, samples, tile):
            wave = jnp.abs(dot_rows(basis_ref[t : t + tile, :], response))
            wave = jnp.max(wave.reshape(tile // 8, 8, wave.shape[1]), axis=0)
            peak = wave if peak is None else jnp.maximum(peak, wave)
        top = jnp.max(peak, axis=0, keepdims=True)
        columns = top.shape[1] // number
        for i in range(number):
            peaks[first + i : first + i + 1, :] = top[:, i * columns : (i + 1) * columns]

    periods = gain_re_ref.shape[0]
    together = 2
    for first in range(0, periods, together):
        some_periods(first, min(together, periods - first))
    peak_ref[...] = peaks[...].T[:, :periods]
    for copy in copies:
        copy.wait()


def vmem():
    return pl.BlockSpec(memory_space=pltpu.VMEM)


def hbm():
    return pl.BlockSpec(memory_space=pltpu.HBM)


def smem():
    return pl.BlockSpec(memory_space=pltpu.SMEM)


def params(mebibytes, held=0):
    return pltpu.CompilerParams(vmem_limit_bytes=mebibytes * 2**20 + held)


def beside(microseconds):
    return pl.CostEstimate(
        flops=microseconds * 10**9, bytes_accessed=microseconds * 3 * 10**6, transcendentals=0
    )


def per_device(sgt, mechanism, slip, point_list, subfault_counts):
    workers = lax.axis_size("sub")
    site_parts = lax.axis_size("site")
    slots, variations, _, freqs = slip.shape
    points, _, components, _, sites, _ = sgt.shape
    total = point_list.shape[0]
    tall = variations // workers
    high = 2 * components * sites // workers
    slip_rows = slots * tall
    proj_rows = points * high
    flat = slip.reshape(slots * variations * 2, freqs)
    packed = pl.pallas_call(
        functools.partial(pack_slip_kernel, workers),
        out_shape=jax.ShapeDtypeStruct((workers, slip_rows + slots, LANES), BF16),
        in_specs=[hbm(), hbm()],
        out_specs=hbm(),
        scratch_shapes=[
            pltpu.VMEM(flat.shape, BF16),
            pltpu.VMEM((STRAINS, slots), F32),
            pltpu.VMEM((workers, slip_rows + slots, LANES), BF16),
            pltpu.VMEM(flat.shape, F32),
            pltpu.VMEM((LANES, LANES), F32),
            pltpu.SemaphoreType.DMA((4,)),
            pltpu.SemaphoreType.DMA,
            pltpu.SemaphoreType.DMA((5,)),
        ],
        compiler_params=params(58),
        name="pack_slip",
    )(flat, mechanism.T)
    own = lax.all_to_all(packed, "sub", split_axis=0, concat_axis=0, tiled=True)
    other = lax.ppermute(own, "site", [(i, i ^ 1) for i in range(site_parts)])
    chosen, starts, lines = pl.pallas_call(
        functools.partial(choose_kernel, workers, tall, high),
        out_shape=(
            jax.ShapeDtypeStruct((points, total), F32),
            jax.ShapeDtypeStruct((total + GROUP + 1,), jnp.int32),
            jax.ShapeDtypeStruct((total + GROUP + 1,), jnp.int32),
        ),
        in_specs=[vmem(), smem(), smem()],
        out_specs=(vmem(), smem(), smem()),
        cost_estimate=beside(10),
        name="choose",
    )(point_list.reshape(1, total), point_list, subfault_counts)
    chosen = chosen.astype(BF16)
    projected = pl.pallas_call(
        functools.partial(project_kernel, workers),
        out_shape=jax.ShapeDtypeStruct((workers, proj_rows, LANES), BF16),
        in_specs=[vmem(), vmem(), vmem()],
        out_specs=vmem(),
        scratch_shapes=[
            pltpu.VMEM((points, LANES), F32),
            pltpu.VMEM((proj_rows * workers, LANES), F32),
        ],
        compiler_params=params(24),
        name="project",
    )(chosen, own, sgt)
    chunks = lax.all_to_all(projected, "sub", split_axis=0, concat_axis=0, tiled=True)
    capacity = total // 2 + GROUP
    spread_bytes = 2 * capacity * variations * LANES * 2
    spread = pl.pallas_call(
        functools.partial(gather_kernel, workers, tall),
        out_shape=jax.ShapeDtypeStruct((2, capacity * variations, LANES), BF16),
        in_specs=[smem(), vmem(), vmem()],
        out_specs=vmem(),
        scratch_shapes=[
            pltpu.VMEM((2, workers * slip_rows, LANES), F32),
            pltpu.VMEM((GROUP, 2, variations, LANES), F32),
        ],
        compiler_params=params(16, spread_bytes),
        name="gather",
    )(lines, own, other)
    partial_rows = tall * high
    spectrum = pl.pallas_call(
        functools.partial(contract_kernel, workers, tall),
        out_shape=jax.ShapeDtypeStruct((workers * partial_rows, LANES), BF16),
        in_specs=[smem(), vmem(), vmem()],
        out_specs=vmem(),
        scratch_shapes=[
            pltpu.VMEM((workers * proj_rows, LANES), F32),
            pltpu.VMEM((3, BLOCK, variations, LANES), F32),
            pltpu.VMEM((3, BLOCK, variations, LANES), F32),
            pltpu.VMEM((3, high // 2, workers, tall, LANES), F32),
            pltpu.VMEM((high * variations, LANES), F32),
            pltpu.VMEM((high * variations, LANES), F32),
        ],
        compiler_params=params(12, spread_bytes),
        name="contract",
    )(starts, spread, chunks)
    basis, basis_rest = pl.pallas_call(
        tables_kernel,
        out_shape=(jax.ShapeDtypeStruct((NT, 2 * freqs), BF16),) * 2,
        in_specs=[vmem()] * 4 + [hbm()],
        out_specs=(vmem(), vmem()),
        compiler_params=params(16),
        name="tables",
    )(*basis_angles(freqs, NT, 64), spectrum)
    gains = oscillator_gains(PERIODS, freqs, NT)
    spectrum = lax.all_to_all(spectrum, "sub", split_axis=0, concat_axis=0, tiled=True)
    width = tall * components * sites
    motion, peaks = pl.pallas_call(
        functools.partial(synthesis_kernel, workers, tall),
        out_shape=(
            jax.ShapeDtypeStruct((width, NT), BF16),
            jax.ShapeDtypeStruct((width, PERIODS), F32),
        ),
        in_specs=[vmem()] * 5,
        out_specs=(hbm(), vmem()),
        scratch_shapes=[
            pltpu.VMEM(spectrum.shape, F32),
            pltpu.VMEM((2 * width, freqs), F32),
            pltpu.VMEM((LANES, width), F32),
            pltpu.VMEM((width, NT), BF16),
            pltpu.SemaphoreType.DMA((4,)),
        ],
        compiler_params=params(32),
        name="synthesis",
    )(spectrum, *gains, basis, basis_rest)
    return (
        motion.reshape(tall, components, sites, NT),
        peaks.reshape(tall, components, sites, PERIODS),
    )


def solution(mesh):
    in_specs = (
        P("sub", None, None, None, "site", None),
        P("sub", None),
        P("sub", None, None, None),
        P(),
        P(),
    )
    out_specs = (P("sub", None, "site", None), P("sub", None, "site", None))
    return jax.shard_map(
        per_device, mesh=mesh, in_specs=in_specs, out_specs=out_specs, check_vma=False
    )
```

```python
import functools
import math

import jax
import jax.numpy as jnp
from jax import lax
from jax.experimental import pallas as pl
from jax.experimental.pallas import tpu as pltpu
from jax.sharding import PartitionSpec as P

NT = 2048
PERIODS = 40

damping = 0.05
sample_step = 0.1

LANES = 128
STRAINS = 6
BLOCK = 4
GROUP = 16
BF16 = jnp.bfloat16
F32 = jnp.float32


def basis_angles(freq_count, sample_count, fine):
    freq_ids = jnp.arange(freq_count, dtype=jnp.int32)
    tables = []
    for time_ids in (jnp.arange(0, sample_count, fine), jnp.arange(fine)):
        angles = (time_ids.astype(jnp.int32)[:, None] * freq_ids[None, :] % sample_count).astype(
            F32
        ) * (2.0 * math.pi / sample_count)
        tables += [jnp.cos(angles), jnp.sin(angles)]
    return tables


def oscillator_gains(period_count, freq_count, sample_count):
    period_ids = jnp.arange(period_count, dtype=F32)
    periods = 2.0 * jnp.exp(period_ids * (math.log(5.0) / max(period_count - 1, 1)))
    natural = 2.0 * math.pi / periods
    omega_bins = jnp.arange(freq_count, dtype=F32) * (2.0 * math.pi / (sample_count * sample_step))
    squared_natural = (natural * natural)[:, None]
    real_part = squared_natural - (omega_bins * omega_bins)[None, :]
    imag_part = 2.0 * damping * natural[:, None] * omega_bins[None, :]
    magnitude = real_part * real_part + imag_part * imag_part
    return (-squared_natural * real_part / magnitude, squared_natural * imag_part / magnitude)


def roll_groups(array, groups, count):
    shift = (groups % count) * (LANES // count)
    return pltpu.roll(array, shift, 1) if shift else array


def swap_blocks(parts):
    count = len(parts)
    group = lax.broadcasted_iota(jnp.int32, parts[0].shape, 1) // (LANES // count)
    step = 1
    while step < count:
        own = (group & step) == 0
        parts = [jnp.where(own, parts[i], parts[(i + step) % count]) for i in range(count)]
        step *= 2
    return [parts[-d % count] for d in range(count)]


def pack_slip_kernel(workers, slip_hbm, mech_hbm, out_hbm, narrow, mech_ref, out_ref, wide, padded, done, mech_done, sent):
    core = lax.rem(lax.axis_index("site"), 2)
    stride = 2 * workers
    slots = mech_ref.shape[1]
    rows = out_ref.shape[1] - slots
    tall = rows // slots
    block = slip_hbm.shape[0] // slots
    pieces = done.shape[0]
    height = rows // pieces
    copies = []
    for i in range(pieces):
        here = pl.ds(i * height * stride, height * stride)
        copies.append(pltpu.make_async_copy(slip_hbm.at[here, :], narrow.at[here, :], done.at[i]))
        copies[i].start()
    mech_copy = pltpu.make_async_copy(mech_hbm, mech_ref, mech_done)
    mech_copy.start()
    padded[...] = jnp.zeros_like(padded)
    mech_copy.wait()
    padded[:STRAINS, :slots] = mech_ref[...]
    moments = padded[...].T[:slots, :]
    first = moments.astype(BF16).astype(F32)
    second = (moments - first).astype(BF16).astype(F32)
    third = moments - first - second
    coded = (
        first + pltpu.roll(second, STRAINS, 1) + pltpu.roll(third, 2 * STRAINS, 1)
    ).astype(BF16)
    for d in range(workers):
        out_ref[d, rows:, :] = coded
    sends = [
        pltpu.make_async_copy(out_ref.at[:, part, :], out_hbm.at[:, part, :], sent.at[i])
        for i, part in enumerate(
            [pl.ds(i * height, height) for i in range(pieces)] + [pl.ds(rows, slots)]
        )
    ]
    sends[pieces].start()
    chunk = 16
    for i in range(pieces):
        copies[i].wait()
        here = pl.ds(i * height * stride, height * stride)
        wide[here, :] = narrow[here, :].astype(F32)
        for start in range(i * height, (i + 1) * height, chunk):
            first = start // tall
            parts = []
            for x in range(workers):
                lines = [
                    wide[pl.ds(j * block + 2 * x * tall + core, tall, stride=2), :]
                    for j in range(first, first + chunk // tall)
                ]
                parts.append(
                    roll_groups(jnp.concatenate(lines, axis=0).astype(BF16), x, workers)
                )
            for d, part in enumerate(swap_blocks(parts)):
                out_ref[d, start : start + chunk, :] = part
        sends[i].start()
    for send in sends:
        send.wait()


def choose_kernel(
    workers, tall, high, point_ref, slots_ref, count_ref, chosen_ref, start_ref, line_ref
):
    points, total = chosen_ref.shape
    slots = total // workers
    point_ids = lax.axis_index("sub") * points + lax.broadcasted_iota(
        jnp.int32, (points, total), 0
    )
    chosen_ref[...] = (point_ref[...] == point_ids).astype(F32)

    def note_worker(w, filled):
        def note_slot(k, carry):
            j = w * slots + k
            start_ref[filled + k] = slots_ref[j] * high
            line_ref[filled + k] = j * tall
            return carry

        count = count_ref[w]
        lax.fori_loop(0, count, note_slot, 0)
        return filled + count

    amount = lax.fori_loop(0, workers, note_worker, 0)
    for extra in range(GROUP):
        start_ref[amount + extra] = 0
        line_ref[amount + extra] = 0
    start_ref[total + GROUP] = (amount + 2 * BLOCK - 1) // (2 * BLOCK)
    line_ref[total + GROUP] = amount


def project_kernel(
    workers, chosen_ref, recv_ref, sgt_ref, out_hbm, out_ref, moments, wide, sent
):
    points = sgt_ref.shape[0]
    sites = sgt_ref.shape[4]
    mech_start = recv_ref.shape[1] - chosen_ref.shape[1] // workers
    coded = jnp.concatenate([recv_ref[w, mech_start:, :] for w in range(workers)], axis=0)
    coded = jnp.dot(chosen_ref[...], coded, preferred_element_type=F32)
    moments[...] = (
        coded + pltpu.roll(coded, LANES - STRAINS, 1) + pltpu.roll(coded, LANES - 2 * STRAINS, 1)
    )
    height = 4 * sites

    def one_point(row):
        moment = moments[pl.ds(row, 1), :]
        weights = [
            jnp.broadcast_to(moment[:, m : m + 1], (sites, LANES)) for m in range(STRAINS)
        ]
        for p in range(2):
            for c in range(2):
                combined = weights[0] * sgt_ref[row, p, c, 0].astype(F32)
                for m in range(1, STRAINS):
                    combined = combined + weights[m] * sgt_ref[row, p, c, m].astype(F32)
                start = pl.multiple_of(row * height + (2 * p + c) * sites, sites)
                wide[pl.ds(start, sites), :] = combined.astype(BF16).astype(F32)

    rows = out_ref.shape[1]
    pieces = sent.shape[0]
    group = 4
    chunk = 16

    def some_points(step, carry):
        for u in range(group):
            one_point(step * group + u)
        return carry

    sends = []
    for i in range(pieces):
        steps = points // pieces // group
        if steps == 1:
            some_points(i, 0)
        else:
            lax.fori_loop(i * steps, (i + 1) * steps, some_points, 0)
        for start in range(i * rows // pieces, (i + 1) * rows // pieces, chunk):
            parts = [
                roll_groups(
                    wide[pl.ds(start * workers + x, chunk, stride=workers), :].astype(BF16),
                    x,
                    workers,
                )
                for x in range(workers)
            ]
            for d, part in enumerate(swap_blocks(parts)):
                out_ref[d, start : start + chunk, :] = part
        here = pl.ds(i * rows // pieces, rows // pieces)
        sends.append(
            pltpu.make_async_copy(out_ref.at[:, here, :], out_hbm.at[:, here, :], sent.at[i])
        )
        sends[i].start()
    for send in sends:
        send.wait()


def gather_kernel(workers, tall, line_ref, own_ref, other_ref, spread_ref, slip, wide):
    core = lax.rem(lax.axis_index("site"), 2)
    total = line_ref.shape[0] - GROUP - 1
    amount = line_ref[total + GROUP]
    slip_rows = total // workers * tall
    height = workers * tall
    for w in range(workers):
        here = slice(w * slip_rows, (w + 1) * slip_rows)
        slip[core, here, :] = own_ref[w, :slip_rows, :].astype(F32)
        slip[1 - core, here, :] = other_ref[w, :slip_rows, :].astype(F32)
    width = LANES // workers
    me = lax.axis_index("sub")
    group = lax.broadcasted_iota(jnp.int32, (tall, LANES), 1) // width
    row_ids = lax.broadcasted_iota(jnp.int32, (LANES, LANES), 0)
    lane_ids = lax.broadcasted_iota(jnp.int32, (LANES, LANES), 1)
    repeat = (row_ids % width == lane_ids % width).astype(F32).astype(BF16)

    def spread_slots(step, carry):
        for i in range(GROUP):
            index = step * GROUP + i
            for p in range(2):
                packed = slip[p, pl.ds(pl.multiple_of(line_ref[index], tall), tall), :]
                for x in range(workers):
                    wide[i, p, x * tall : (x + 1) * tall, :] = jnp.where(
                        (group == lax.rem(x + me, workers)) & (index < amount), packed, 0.0
                    )
        for i in range(GROUP):
            start = pl.multiple_of((step * GROUP + i) * height, height)
            for p in range(2):
                spread_ref[p, pl.ds(start, height), :] = jnp.dot(
                    wide[i, p].astype(BF16), repeat, preferred_element_type=F32
                ).astype(BF16)
        return carry

    lax.fori_loop(0, (amount + GROUP - 1) // GROUP, spread_slots, 0)


def contract_kernel(
    workers, tall, start_ref, spread_ref, proj_ref, out_ref, proj, even, odd, total, outgoing
):
    proj_rows = proj_ref.shape[1]
    high = outgoing.shape[0] // (workers * tall)
    half = high // 2
    variations = workers * tall
    lines = min(2, half)
    for w in range(workers):
        proj[w * proj_rows : (w + 1) * proj_rows, :] = proj_ref[w].astype(F32)
    total[...] = jnp.zeros_like(total)

    def widen_block(first, spread):
        for i in range(BLOCK):
            here = pl.ds(pl.multiple_of((first + i) * variations, variations), variations)
            real = spread_ref[0, here, :].astype(F32)
            imag = spread_ref[1, here, :].astype(F32)
            spread[0, i] = real + imag
            spread[1, i] = imag
            spread[2, i] = real

    def add_block(first, spread):
        starts = [start_ref[first + i] for i in range(BLOCK)]
        for line in range(0, half, lines):
            green = []
            for i in range(BLOCK):
                for y in range(line, line + lines):
                    real = jnp.broadcast_to(proj[pl.ds(starts[i] + y, 1), :], (tall, LANES))
                    imag = jnp.broadcast_to(proj[pl.ds(starts[i] + half + y, 1), :], (tall, LANES))
                    green.append((real, real + imag, imag - real))
            for x in range(workers):
                sums = [
                    [total[kind, y, x] for kind in range(3)] for y in range(line, line + lines)
                ]
                for i in range(BLOCK):
                    factors = [spread[kind, i, x * tall : (x + 1) * tall, :] for kind in range(3)]
                    for y in range(lines):
                        for kind in range(3):
                            sums[y][kind] = (
                                sums[y][kind] + green[i * lines + y][kind] * factors[kind]
                            )
                for y in range(lines):
                    for kind in range(3):
                        total[kind, line + y, x] = sums[y][kind]

    def add_two_blocks(step, carry):
        first = step * (2 * BLOCK)
        widen_block(first, even)
        widen_block(first + BLOCK, odd)
        add_block(first, even)
        add_block(first + BLOCK, odd)
        return carry

    lax.fori_loop(0, start_ref[start_ref.shape[0] - 1], add_two_blocks, 0)
    for y in range(half):
        for x in range(workers):
            shared = total[0, y, x]
            at_real = (x * high + y) * tall
            at_imag = (x * high + half + y) * tall
            outgoing[at_real : at_real + tall, :] = shared - total[1, y, x]
            outgoing[at_imag : at_imag + tall, :] = shared + total[2, y, x]
    out_ref[...] = outgoing[...].astype(BF16)


def dot_rows(a, b):
    return lax.dot_general(a, b, (((1,), (1,)), ((), ())), preferred_element_type=F32)


def tables_kernel(
    coarse_cos_ref, coarse_sin_ref, fine_cos_ref, fine_sin_ref, ready_hbm, basis_ref, rest_ref
):
    del ready_hbm
    fine, freqs = fine_cos_ref.shape
    norm_scale = 1.0 / math.sqrt(freqs)
    cosine = norm_scale * fine_cos_ref[...]
    sine = norm_scale * fine_sin_ref[...]
    for i in range(coarse_cos_ref.shape[0]):
        start_cos, start_sin = coarse_cos_ref[i : i + 1, :], coarse_sin_ref[i : i + 1, :]
        here = slice(i * fine, (i + 1) * fine)
        for part, values in enumerate(
            (start_cos * cosine - start_sin * sine, -(start_sin * cosine) - start_cos * sine)
        ):
            low = values.astype(BF16)
            basis_ref[here, part * freqs : (part + 1) * freqs] = low
            rest_ref[here, part * freqs : (part + 1) * freqs] = (
                values - low.astype(F32)
            ).astype(BF16)


def synthesis_kernel(
    workers,
    tall,
    recv_ref,
    gain_re_ref,
    gain_im_ref,
    basis_ref,
    rest_ref,
    motion_hbm,
    peak_ref,
    received,
    natural,
    peaks,
    motion_ref,
    done,
):
    freqs = natural.shape[1]
    rows = recv_ref.shape[0] // workers
    high = rows // tall
    if rows % 16:
        received[...] = recv_ref[...].astype(F32)
        parts = [received[w * rows : (w + 1) * rows, :] for w in range(workers)]
    else:
        parts = [recv_ref[w * rows : (w + 1) * rows, :] for w in range(workers)]
    for x, part in enumerate(swap_blocks(parts)):
        part = roll_groups(part, -x, workers).astype(F32)
        for r in range(high):
            start = (r * workers + x) * tall
            natural[start : start + tall, :] = part[r * tall : (r + 1) * tall, :]
    real, imag = [
        jnp.concatenate(
            [
                natural[pl.ds(r * workers * tall + v, workers, stride=tall), :]
                for v in range(tall)
                for r in range(first, first + high // 2)
            ],
            axis=0,
        )
        for first in (0, high // 2)
    ]
    spectrum = jnp.concatenate([real.astype(BF16), imag.astype(BF16)], axis=1)
    samples = basis_ref.shape[0]
    tile = samples // 4
    copies = []
    for i in range(4):
        here = slice(i * tile, (i + 1) * tile)
        motion = dot_rows(spectrum, basis_ref[here, :]) + dot_rows(spectrum, rest_ref[here, :])
        motion_ref[:, here] = motion.astype(BF16)
        copies.append(
            pltpu.make_async_copy(motion_ref.at[:, here], motion_hbm.at[:, here], done.at[i])
        )
        copies[i].start()

    def response_of(q):
        gain_re = gain_re_ref[q : q + 1, :]
        gain_im = gain_im_ref[q : q + 1, :]
        return jnp.concatenate(
            [
                (gain_re * real - gain_im * imag).astype(BF16),
                (gain_re * imag + gain_im * real).astype(BF16),
            ],
            axis=1,
        )

    def some_periods(first, number):
        response = jnp.concatenate([response_of(first + i) for i in range(number)], axis=0)
        peak = None
        for t in range(0, samples, tile):
            wave = jnp.abs(dot_rows(basis_ref[t : t + tile, :], response))
            wave = jnp.max(wave.reshape(tile // 8, 8, wave.shape[1]), axis=0)
            peak = wave if peak is None else jnp.maximum(peak, wave)
        top = jnp.max(peak, axis=0, keepdims=True)
        columns = top.shape[1] // number
        for i in range(number):
            peaks[first + i : first + i + 1, :] = top[:, i * columns : (i + 1) * columns]

    periods = gain_re_ref.shape[0]
    together = 2
    for first in range(0, periods, together):
        some_periods(first, min(together, periods - first))
    peak_ref[...] = peaks[...].T[:, :periods]
    for copy in copies:
        copy.wait()


def vmem():
    return pl.BlockSpec(memory_space=pltpu.VMEM)


def hbm():
    return pl.BlockSpec(memory_space=pltpu.HBM)


def smem():
    return pl.BlockSpec(memory_space=pltpu.SMEM)


def params(mebibytes, held=0):
    return pltpu.CompilerParams(vmem_limit_bytes=mebibytes * 2**20 + held)


def beside(microseconds):
    return pl.CostEstimate(
        flops=microseconds * 10**9, bytes_accessed=microseconds * 3 * 10**6, transcendentals=0
    )


def per_device(sgt, mechanism, slip, point_list, subfault_counts):
    workers = lax.axis_size("sub")
    site_parts = lax.axis_size("site")
    slots, variations, _, freqs = slip.shape
    points, _, components, _, sites, _ = sgt.shape
    total = point_list.shape[0]
    tall = variations // workers
    high = 2 * components * sites // workers
    slip_rows = slots * tall
    proj_rows = points * high
    flat = slip.reshape(slots * variations * 2, freqs)
    packed = pl.pallas_call(
        functools.partial(pack_slip_kernel, workers),
        out_shape=jax.ShapeDtypeStruct((workers, slip_rows + slots, LANES), BF16),
        in_specs=[hbm(), hbm()],
        out_specs=hbm(),
        scratch_shapes=[
            pltpu.VMEM(flat.shape, BF16),
            pltpu.VMEM((STRAINS, slots), F32),
            pltpu.VMEM((workers, slip_rows + slots, LANES), BF16),
            pltpu.VMEM(flat.shape, F32),
            pltpu.VMEM((LANES, LANES), F32),
            pltpu.SemaphoreType.DMA((4,)),
            pltpu.SemaphoreType.DMA,
            pltpu.SemaphoreType.DMA((5,)),
        ],
        compiler_params=params(58),
        name="pack_slip",
    )(flat, mechanism.T)
    own = lax.all_to_all(packed, "sub", split_axis=0, concat_axis=0, tiled=True)
    other = lax.ppermute(own, "site", [(i, i ^ 1) for i in range(site_parts)])
    chosen, starts, lines = pl.pallas_call(
        functools.partial(choose_kernel, workers, tall, high),
        out_shape=(
            jax.ShapeDtypeStruct((points, total), F32),
            jax.ShapeDtypeStruct((total + GROUP + 1,), jnp.int32),
            jax.ShapeDtypeStruct((total + GROUP + 1,), jnp.int32),
        ),
        in_specs=[vmem(), smem(), smem()],
        out_specs=(vmem(), smem(), smem()),
        cost_estimate=beside(10),
        name="choose",
    )(point_list.reshape(1, total), point_list, subfault_counts)
    chosen = chosen.astype(BF16)
    projected = pl.pallas_call(
        functools.partial(project_kernel, workers),
        out_shape=jax.ShapeDtypeStruct((workers, proj_rows, LANES), BF16),
        in_specs=[vmem(), vmem(), vmem()],
        out_specs=hbm(),
        scratch_shapes=[
            pltpu.VMEM((workers, proj_rows, LANES), BF16),
            pltpu.VMEM((points, LANES), F32),
            pltpu.VMEM((proj_rows * workers, LANES), F32),
            pltpu.SemaphoreType.DMA((4,)),
        ],
        compiler_params=params(24),
        name="project",
    )(chosen, own, sgt)
    chunks = lax.all_to_all(projected, "sub", split_axis=0, concat_axis=0, tiled=True)
    capacity = total // 2 + GROUP
    spread_bytes = 2 * capacity * variations * LANES * 2
    spread = pl.pallas_call(
        functools.partial(gather_kernel, workers, tall),
        out_shape=jax.ShapeDtypeStruct((2, capacity * variations, LANES), BF16),
        in_specs=[smem(), vmem(), vmem()],
        out_specs=vmem(),
        scratch_shapes=[
            pltpu.VMEM((2, workers * slip_rows, LANES), F32),
            pltpu.VMEM((GROUP, 2, variations, LANES), F32),
        ],
        compiler_params=params(16, spread_bytes),
        name="gather",
    )(lines, own, other)
    partial_rows = tall * high
    spectrum = pl.pallas_call(
        functools.partial(contract_kernel, workers, tall),
        out_shape=jax.ShapeDtypeStruct((workers * partial_rows, LANES), BF16),
        in_specs=[smem(), vmem(), vmem()],
        out_specs=vmem(),
        scratch_shapes=[
            pltpu.VMEM((workers * proj_rows, LANES), F32),
            pltpu.VMEM((3, BLOCK, variations, LANES), F32),
            pltpu.VMEM((3, BLOCK, variations, LANES), F32),
            pltpu.VMEM((3, high // 2, workers, tall, LANES), F32),
            pltpu.VMEM((high * variations, LANES), F32),
        ],
        compiler_params=params(12, spread_bytes),
        name="contract",
    )(starts, spread, chunks)
    basis, basis_rest = pl.pallas_call(
        tables_kernel,
        out_shape=(jax.ShapeDtypeStruct((NT, 2 * freqs), BF16),) * 2,
        in_specs=[vmem()] * 4 + [hbm()],
        out_specs=(vmem(), vmem()),
        compiler_params=params(16),
        name="tables",
    )(*basis_angles(freqs, NT, 64), spectrum)
    gains = oscillator_gains(PERIODS, freqs, NT)
    spectrum = lax.all_to_all(spectrum, "sub", split_axis=0, concat_axis=0, tiled=True)
    width = tall * components * sites
    motion, peaks = pl.pallas_call(
        functools.partial(synthesis_kernel, workers, tall),
        out_shape=(
            jax.ShapeDtypeStruct((width, NT), BF16),
            jax.ShapeDtypeStruct((width, PERIODS), F32),
        ),
        in_specs=[vmem()] * 5,
        out_specs=(hbm(), vmem()),
        scratch_shapes=[
            pltpu.VMEM(spectrum.shape, F32),
            pltpu.VMEM((2 * width, freqs), F32),
            pltpu.VMEM((LANES, width), F32),
            pltpu.VMEM((width, NT), BF16),
            pltpu.SemaphoreType.DMA((4,)),
        ],
        compiler_params=params(32),
        name="synthesis",
    )(spectrum, *gains, basis, basis_rest)
    return (
        motion.reshape(tall, components, sites, NT),
        peaks.reshape(tall, components, sites, PERIODS),
    )


def solution(mesh):
    in_specs = (
        P("sub", None, None, None, "site", None),
        P("sub", None),
        P("sub", None, None, None),
        P(),
        P(),
    )
    out_specs = (P("sub", None, "site", None), P("sub", None, "site", None))
    return jax.shard_map(
        per_device, mesh=mesh, in_specs=in_specs, out_specs=out_specs, check_vma=False
    )
```

```python
import functools
import math

import jax
import jax.numpy as jnp
from jax import lax
from jax.experimental import pallas as pl
from jax.experimental.pallas import tpu as pltpu
from jax.sharding import PartitionSpec as P

NT = 2048
PERIODS = 40

damping = 0.05
sample_step = 0.1

LANES = 128
STRAINS = 6
BLOCK = 4
GROUP = 16
BF16 = jnp.bfloat16
F32 = jnp.float32


def basis_angles(freq_count, sample_count, fine):
    freq_ids = jnp.arange(freq_count, dtype=jnp.int32)
    tables = []
    for time_ids in (jnp.arange(0, sample_count, fine), jnp.arange(fine)):
        angles = (time_ids.astype(jnp.int32)[:, None] * freq_ids[None, :] % sample_count).astype(
            F32
        ) * (2.0 * math.pi / sample_count)
        tables += [jnp.cos(angles), jnp.sin(angles)]
    return tables


def oscillator_gains(period_count, freq_count, sample_count):
    period_ids = jnp.arange(period_count, dtype=F32)
    periods = 2.0 * jnp.exp(period_ids * (math.log(5.0) / max(period_count - 1, 1)))
    natural = 2.0 * math.pi / periods
    omega_bins = jnp.arange(freq_count, dtype=F32) * (2.0 * math.pi / (sample_count * sample_step))
    squared_natural = (natural * natural)[:, None]
    real_part = squared_natural - (omega_bins * omega_bins)[None, :]
    imag_part = 2.0 * damping * natural[:, None] * omega_bins[None, :]
    magnitude = real_part * real_part + imag_part * imag_part
    return (-squared_natural * real_part / magnitude, squared_natural * imag_part / magnitude)


def roll_groups(array, groups, count):
    shift = (groups % count) * (LANES // count)
    return pltpu.roll(array, shift, 1) if shift else array


def swap_blocks(parts):
    count = len(parts)
    group = lax.broadcasted_iota(jnp.int32, parts[0].shape, 1) // (LANES // count)
    step = 1
    while step < count:
        own = (group & step) == 0
        parts = [jnp.where(own, parts[i], parts[(i + step) % count]) for i in range(count)]
        step *= 2
    return [parts[-d % count] for d in range(count)]


def pack_slip_kernel(workers, slip_hbm, mech_hbm, out_hbm, narrow, mech_ref, out_ref, wide, padded, done, mech_done, sent):
    core = lax.rem(lax.axis_index("site"), 2)
    stride = 2 * workers
    slots = mech_ref.shape[1]
    rows = out_ref.shape[1] - slots
    tall = rows // slots
    block = slip_hbm.shape[0] // slots
    pieces = done.shape[0]
    height = rows // pieces
    copies = []
    for i in range(pieces):
        here = pl.ds(i * height * stride, height * stride)
        copies.append(pltpu.make_async_copy(slip_hbm.at[here, :], narrow.at[here, :], done.at[i]))
        copies[i].start()
    mech_copy = pltpu.make_async_copy(mech_hbm, mech_ref, mech_done)
    mech_copy.start()
    padded[...] = jnp.zeros_like(padded)
    mech_copy.wait()
    padded[:STRAINS, :slots] = mech_ref[...]
    moments = padded[...].T[:slots, :]
    first = moments.astype(BF16).astype(F32)
    second = (moments - first).astype(BF16).astype(F32)
    third = moments - first - second
    coded = (
        first + pltpu.roll(second, STRAINS, 1) + pltpu.roll(third, 2 * STRAINS, 1)
    ).astype(BF16)
    for d in range(workers):
        out_ref[d, rows:, :] = coded
    sends = [
        pltpu.make_async_copy(out_ref.at[:, part, :], out_hbm.at[:, part, :], sent.at[i])
        for i, part in enumerate(
            [pl.ds(i * height, height) for i in range(pieces)] + [pl.ds(rows, slots)]
        )
    ]
    sends[pieces].start()
    chunk = 16
    for i in range(pieces):
        copies[i].wait()
        here = pl.ds(i * height * stride, height * stride)
        wide[here, :] = narrow[here, :].astype(F32)
        for start in range(i * height, (i + 1) * height, chunk):
            first = start // tall
            parts = []
            for x in range(workers):
                lines = [
                    wide[pl.ds(j * block + 2 * x * tall + core, tall, stride=2), :]
                    for j in range(first, first + chunk // tall)
                ]
                parts.append(
                    roll_groups(jnp.concatenate(lines, axis=0).astype(BF16), x, workers)
                )
            for d, part in enumerate(swap_blocks(parts)):
                out_ref[d, start : start + chunk, :] = part
        sends[i].start()
    for send in sends:
        send.wait()


def choose_kernel(
    workers, tall, high, point_ref, slots_ref, count_ref, chosen_ref, start_ref, line_ref
):
    points, total = chosen_ref.shape
    slots = total // workers
    point_ids = lax.axis_index("sub") * points + lax.broadcasted_iota(
        jnp.int32, (points, total), 0
    )
    chosen_ref[...] = (point_ref[...] == point_ids).astype(F32)

    def note_worker(w, filled):
        def note_slot(k, carry):
            j = w * slots + k
            start_ref[filled + k] = slots_ref[j] * high
            line_ref[filled + k] = j * tall
            return carry

        count = count_ref[w]
        lax.fori_loop(0, count, note_slot, 0)
        return filled + count

    amount = lax.fori_loop(0, workers, note_worker, 0)
    for extra in range(GROUP):
        start_ref[amount + extra] = 0
        line_ref[amount + extra] = 0
    start_ref[total + GROUP] = (amount + 2 * BLOCK - 1) // (2 * BLOCK)
    line_ref[total + GROUP] = amount


def project_kernel(
    workers, chosen_ref, recv_ref, sgt_ref, out_hbm, out_ref, moments, wide, sent
):
    points = sgt_ref.shape[0]
    sites = sgt_ref.shape[4]
    mech_start = recv_ref.shape[1] - chosen_ref.shape[1] // workers
    coded = jnp.concatenate([recv_ref[w, mech_start:, :] for w in range(workers)], axis=0)
    coded = jnp.dot(chosen_ref[...], coded, preferred_element_type=F32)
    moments[...] = (
        coded + pltpu.roll(coded, LANES - STRAINS, 1) + pltpu.roll(coded, LANES - 2 * STRAINS, 1)
    )
    height = 4 * sites

    def one_point(row):
        moment = moments[pl.ds(row, 1), :]
        weights = [
            jnp.broadcast_to(moment[:, m : m + 1], (sites, LANES)) for m in range(STRAINS)
        ]
        for p in range(2):
            for c in range(2):
                combined = weights[0] * sgt_ref[row, p, c, 0].astype(F32)
                for m in range(1, STRAINS):
                    combined = combined + weights[m] * sgt_ref[row, p, c, m].astype(F32)
                start = pl.multiple_of(row * height + (2 * p + c) * sites, sites)
                wide[pl.ds(start, sites), :] = combined.astype(BF16).astype(F32)

    rows = out_ref.shape[1]
    pieces = sent.shape[0]
    group = 4
    chunk = 16

    def some_points(step, carry):
        for u in range(group):
            one_point(step * group + u)
        return carry

    sends = []
    for i in range(pieces):
        steps = points // pieces // group
        if steps == 1:
            some_points(i, 0)
        else:
            lax.fori_loop(i * steps, (i + 1) * steps, some_points, 0)
        for start in range(i * rows // pieces, (i + 1) * rows // pieces, chunk):
            parts = [
                roll_groups(
                    wide[pl.ds(start * workers + x, chunk, stride=workers), :].astype(BF16),
                    x,
                    workers,
                )
                for x in range(workers)
            ]
            for d, part in enumerate(swap_blocks(parts)):
                out_ref[d, start : start + chunk, :] = part
        here = pl.ds(i * rows // pieces, rows // pieces)
        sends.append(
            pltpu.make_async_copy(out_ref.at[:, here, :], out_hbm.at[:, here, :], sent.at[i])
        )
        sends[i].start()
    for send in sends:
        send.wait()


def gather_kernel(workers, tall, line_ref, own_ref, other_ref, spread_ref, slip, wide):
    core = lax.rem(lax.axis_index("site"), 2)
    total = line_ref.shape[0] - GROUP - 1
    amount = line_ref[total + GROUP]
    slip_rows = total // workers * tall
    height = workers * tall
    for w in range(workers):
        here = slice(w * slip_rows, (w + 1) * slip_rows)
        slip[core, here, :] = own_ref[w, :slip_rows, :].astype(F32)
        slip[1 - core, here, :] = other_ref[w, :slip_rows, :].astype(F32)
    width = LANES // workers
    me = lax.axis_index("sub")
    group = lax.broadcasted_iota(jnp.int32, (tall, LANES), 1) // width
    row_ids = lax.broadcasted_iota(jnp.int32, (LANES, LANES), 0)
    lane_ids = lax.broadcasted_iota(jnp.int32, (LANES, LANES), 1)
    repeat = (row_ids % width == lane_ids % width).astype(F32).astype(BF16)

    def spread_slots(step, carry):
        for i in range(GROUP):
            index = step * GROUP + i
            for p in range(2):
                packed = slip[p, pl.ds(pl.multiple_of(line_ref[index], tall), tall), :]
                for x in range(workers):
                    wide[i, p, x * tall : (x + 1) * tall, :] = jnp.where(
                        (group == lax.rem(x + me, workers)) & (index < amount), packed, 0.0
                    )
        for i in range(GROUP):
            start = pl.multiple_of((step * GROUP + i) * height, height)
            for p in range(2):
                spread_ref[p, pl.ds(start, height), :] = jnp.dot(
                    wide[i, p].astype(BF16), repeat, preferred_element_type=F32
                ).astype(BF16)
        return carry

    lax.fori_loop(0, (amount + GROUP - 1) // GROUP, spread_slots, 0)


def contract_kernel(
    workers, tall, start_ref, spread_ref, proj_ref, out_ref, proj, even, odd, total, outgoing
):
    proj_rows = proj_ref.shape[1]
    high = outgoing.shape[0] // (workers * tall)
    half = high // 2
    variations = workers * tall
    lines = min(2, half)
    for w in range(workers):
        proj[w * proj_rows : (w + 1) * proj_rows, :] = proj_ref[w].astype(F32)
    total[...] = jnp.zeros_like(total)

    def widen_block(first, spread):
        for i in range(BLOCK):
            here = pl.ds(pl.multiple_of((first + i) * variations, variations), variations)
            real = spread_ref[0, here, :].astype(F32)
            imag = spread_ref[1, here, :].astype(F32)
            spread[0, i] = real + imag
            spread[1, i] = imag
            spread[2, i] = real

    def add_block(first, spread):
        starts = [start_ref[first + i] for i in range(BLOCK)]
        for line in range(0, half, lines):
            green = []
            for i in range(BLOCK):
                for y in range(line, line + lines):
                    real = jnp.broadcast_to(proj[pl.ds(starts[i] + y, 1), :], (tall, LANES))
                    imag = jnp.broadcast_to(proj[pl.ds(starts[i] + half + y, 1), :], (tall, LANES))
                    green.append((real, real + imag, imag - real))
            for x in range(workers):
                sums = [
                    [total[kind, y, x] for kind in range(3)] for y in range(line, line + lines)
                ]
                for i in range(BLOCK):
                    factors = [spread[kind, i, x * tall : (x + 1) * tall, :] for kind in range(3)]
                    for y in range(lines):
                        for kind in range(3):
                            sums[y][kind] = (
                                sums[y][kind] + green[i * lines + y][kind] * factors[kind]
                            )
                for y in range(lines):
                    for kind in range(3):
                        total[kind, line + y, x] = sums[y][kind]

    def add_two_blocks(step, carry):
        first = step * (2 * BLOCK)
        widen_block(first, even)
        widen_block(first + BLOCK, odd)
        add_block(first, even)
        add_block(first + BLOCK, odd)
        return carry

    lax.fori_loop(0, start_ref[start_ref.shape[0] - 1], add_two_blocks, 0)
    for y in range(half):
        for x in range(workers):
            shared = total[0, y, x]
            at_real = (x * high + y) * tall
            at_imag = (x * high + half + y) * tall
            outgoing[at_real : at_real + tall, :] = shared - total[1, y, x]
            outgoing[at_imag : at_imag + tall, :] = shared + total[2, y, x]
    out_ref[...] = outgoing[...].astype(BF16)


def dot_rows(a, b):
    return lax.dot_general(a, b, (((1,), (1,)), ((), ())), preferred_element_type=F32)


def tables_kernel(
    coarse_cos_ref, coarse_sin_ref, fine_cos_ref, fine_sin_ref, ready_hbm, basis_ref, rest_ref
):
    del ready_hbm
    fine, freqs = fine_cos_ref.shape
    norm_scale = 1.0 / math.sqrt(freqs)
    cosine = norm_scale * fine_cos_ref[...]
    sine = norm_scale * fine_sin_ref[...]
    for i in range(coarse_cos_ref.shape[0]):
        start_cos, start_sin = coarse_cos_ref[i : i + 1, :], coarse_sin_ref[i : i + 1, :]
        here = slice(i * fine, (i + 1) * fine)
        for part, values in enumerate(
            (start_cos * cosine - start_sin * sine, -(start_sin * cosine) - start_cos * sine)
        ):
            low = values.astype(BF16)
            basis_ref[here, part * freqs : (part + 1) * freqs] = low
            rest_ref[here, part * freqs : (part + 1) * freqs] = (
                values - low.astype(F32)
            ).astype(BF16)


def synthesis_kernel(
    workers,
    tall,
    recv_ref,
    gain_re_ref,
    gain_im_ref,
    basis_ref,
    rest_ref,
    motion_hbm,
    peak_ref,
    received,
    natural,
    peaks,
    motion_ref,
    done,
):
    freqs = natural.shape[1]
    rows = recv_ref.shape[0] // workers
    high = rows // tall
    if rows % 16:
        received[...] = recv_ref[...].astype(F32)
        parts = [received[w * rows : (w + 1) * rows, :] for w in range(workers)]
    else:
        parts = [recv_ref[w * rows : (w + 1) * rows, :] for w in range(workers)]
    for x, part in enumerate(swap_blocks(parts)):
        part = roll_groups(part, -x, workers).astype(F32)
        for r in range(high):
            start = (r * workers + x) * tall
            natural[start : start + tall, :] = part[r * tall : (r + 1) * tall, :]
    real, imag = [
        jnp.concatenate(
            [
                natural[pl.ds(r * workers * tall + v, workers, stride=tall), :]
                for v in range(tall)
                for r in range(first, first + high // 2)
            ],
            axis=0,
        )
        for first in (0, high // 2)
    ]
    spectrum = jnp.concatenate([real.astype(BF16), imag.astype(BF16)], axis=1)
    samples = basis_ref.shape[0]
    tile = samples // 4
    copies = []
    for i in range(4):
        here = slice(i * tile, (i + 1) * tile)
        motion = dot_rows(spectrum, basis_ref[here, :]) + dot_rows(spectrum, rest_ref[here, :])
        motion_ref[:, here] = motion.astype(BF16)
        copies.append(
            pltpu.make_async_copy(motion_ref.at[:, here], motion_hbm.at[:, here], done.at[i])
        )
        copies[i].start()

    def response_of(q):
        gain_re = gain_re_ref[q : q + 1, :]
        gain_im = gain_im_ref[q : q + 1, :]
        return jnp.concatenate(
            [
                (gain_re * real - gain_im * imag).astype(BF16),
                (gain_re * imag + gain_im * real).astype(BF16),
            ],
            axis=1,
        )

    def some_periods(first, number):
        response = jnp.concatenate([response_of(first + i) for i in range(number)], axis=0)
        peak = None
        for t in range(0, samples, tile):
            wave = jnp.abs(dot_rows(basis_ref[t : t + tile, :], response))
            wave = jnp.max(wave.reshape(tile // 8, 8, wave.shape[1]), axis=0)
            peak = wave if peak is None else jnp.maximum(peak, wave)
        top = jnp.max(peak, axis=0, keepdims=True)
        columns = top.shape[1] // number
        for i in range(number):
            peaks[first + i : first + i + 1, :] = top[:, i * columns : (i + 1) * columns]

    periods = gain_re_ref.shape[0]
    together = 2
    for first in range(0, periods, together):
        some_periods(first, min(together, periods - first))
    peak_ref[...] = peaks[...].T[:, :periods]
    for copy in copies:
        copy.wait()


def vmem():
    return pl.BlockSpec(memory_space=pltpu.VMEM)


def hbm():
    return pl.BlockSpec(memory_space=pltpu.HBM)


def smem():
    return pl.BlockSpec(memory_space=pltpu.SMEM)


def params(mebibytes, held=0):
    return pltpu.CompilerParams(vmem_limit_bytes=mebibytes * 2**20 + held)


def beside(microseconds):
    return pl.CostEstimate(
        flops=microseconds * 10**9, bytes_accessed=microseconds * 3 * 10**6, transcendentals=0
    )


def per_device(sgt, mechanism, slip, point_list, subfault_counts):
    workers = lax.axis_size("sub")
    site_parts = lax.axis_size("site")
    slots, variations, _, freqs = slip.shape
    points, _, components, _, sites, _ = sgt.shape
    total = point_list.shape[0]
    tall = variations // workers
    high = 2 * components * sites // workers
    slip_rows = slots * tall
    proj_rows = points * high
    flat = slip.reshape(slots * variations * 2, freqs)
    packed = pl.pallas_call(
        functools.partial(pack_slip_kernel, workers),
        out_shape=jax.ShapeDtypeStruct((workers, slip_rows + slots, LANES), BF16),
        in_specs=[hbm(), hbm()],
        out_specs=hbm(),
        scratch_shapes=[
            pltpu.VMEM(flat.shape, BF16),
            pltpu.VMEM((STRAINS, slots), F32),
            pltpu.VMEM((workers, slip_rows + slots, LANES), BF16),
            pltpu.VMEM((flat.shape[0] + 2 * tall, freqs), F32),
            pltpu.VMEM((LANES, LANES), F32),
            pltpu.SemaphoreType.DMA((4,)),
            pltpu.SemaphoreType.DMA,
            pltpu.SemaphoreType.DMA((5,)),
        ],
        compiler_params=params(58),
        name="pack_slip",
    )(flat, mechanism.T)
    own = lax.all_to_all(packed, "sub", split_axis=0, concat_axis=0, tiled=True)
    other = lax.ppermute(own, "site", [(i, i ^ 1) for i in range(site_parts)])
    chosen, starts, lines = pl.pallas_call(
        functools.partial(choose_kernel, workers, tall, high),
        out_shape=(
            jax.ShapeDtypeStruct((points, total), F32),
            jax.ShapeDtypeStruct((total + GROUP + 1,), jnp.int32),
            jax.ShapeDtypeStruct((total + GROUP + 1,), jnp.int32),
        ),
        in_specs=[vmem(), smem(), smem()],
        out_specs=(vmem(), smem(), smem()),
        cost_estimate=beside(10),
        name="choose",
    )(point_list.reshape(1, total), point_list, subfault_counts)
    chosen = chosen.astype(BF16)
    projected = pl.pallas_call(
        functools.partial(project_kernel, workers),
        out_shape=jax.ShapeDtypeStruct((workers, proj_rows, LANES), BF16),
        in_specs=[vmem(), vmem(), vmem()],
        out_specs=hbm(),
        scratch_shapes=[
            pltpu.VMEM((workers, proj_rows, LANES), BF16),
            pltpu.VMEM((points, LANES), F32),
            pltpu.VMEM((proj_rows * workers + workers, LANES), F32),
            pltpu.SemaphoreType.DMA((4,)),
        ],
        compiler_params=params(24),
        name="project",
    )(chosen, own, sgt)
    chunks = lax.all_to_all(projected, "sub", split_axis=0, concat_axis=0, tiled=True)
    capacity = total // 2 + GROUP
    spread_bytes = 2 * capacity * variations * LANES * 2
    spread = pl.pallas_call(
        functools.partial(gather_kernel, workers, tall),
        out_shape=jax.ShapeDtypeStruct((2, capacity * variations, LANES), BF16),
        in_specs=[smem(), vmem(), vmem()],
        out_specs=vmem(),
        scratch_shapes=[
            pltpu.VMEM((2, workers * slip_rows, LANES), F32),
            pltpu.VMEM((GROUP, 2, variations, LANES), F32),
        ],
        compiler_params=params(16, spread_bytes),
        name="gather",
    )(lines, own, other)
    partial_rows = tall * high
    spectrum = pl.pallas_call(
        functools.partial(contract_kernel, workers, tall),
        out_shape=jax.ShapeDtypeStruct((workers * partial_rows, LANES), BF16),
        in_specs=[smem(), vmem(), vmem()],
        out_specs=vmem(),
        scratch_shapes=[
            pltpu.VMEM((workers * proj_rows, LANES), F32),
            pltpu.VMEM((3, BLOCK, variations, LANES), F32),
            pltpu.VMEM((3, BLOCK, variations, LANES), F32),
            pltpu.VMEM((3, high // 2, workers, tall, LANES), F32),
            pltpu.VMEM((high * variations, LANES), F32),
        ],
        compiler_params=params(12, spread_bytes),
        name="contract",
    )(starts, spread, chunks)
    basis, basis_rest = pl.pallas_call(
        tables_kernel,
        out_shape=(jax.ShapeDtypeStruct((NT, 2 * freqs), BF16),) * 2,
        in_specs=[vmem()] * 4 + [hbm()],
        out_specs=(vmem(), vmem()),
        compiler_params=params(16),
        name="tables",
    )(*basis_angles(freqs, NT, 64), spectrum)
    gains = oscillator_gains(PERIODS, freqs, NT)
    spectrum = lax.all_to_all(spectrum, "sub", split_axis=0, concat_axis=0, tiled=True)
    width = tall * components * sites
    motion, peaks = pl.pallas_call(
        functools.partial(synthesis_kernel, workers, tall),
        out_shape=(
            jax.ShapeDtypeStruct((width, NT), BF16),
            jax.ShapeDtypeStruct((width, PERIODS), F32),
        ),
        in_specs=[vmem()] * 5,
        out_specs=(hbm(), vmem()),
        scratch_shapes=[
            pltpu.VMEM(spectrum.shape, F32),
            pltpu.VMEM((2 * width + workers, freqs), F32),
            pltpu.VMEM((LANES, width), F32),
            pltpu.VMEM((width, NT), BF16),
            pltpu.SemaphoreType.DMA((4,)),
        ],
        compiler_params=params(32),
        name="synthesis",
    )(spectrum, *gains, basis, basis_rest)
    return (
        motion.reshape(tall, components, sites, NT),
        peaks.reshape(tall, components, sites, PERIODS),
    )


def solution(mesh):
    in_specs = (
        P("sub", None, None, None, "site", None),
        P("sub", None),
        P("sub", None, None, None),
        P(),
        P(),
    )
    out_specs = (P("sub", None, "site", None), P("sub", None, "site", None))
    return jax.shard_map(
        per_device, mesh=mesh, in_specs=in_specs, out_specs=out_specs, check_vma=False
    )
```

```python
import functools
import math

import jax
import jax.numpy as jnp
from jax import lax
from jax.experimental import pallas as pl
from jax.experimental.pallas import tpu as pltpu
from jax.sharding import PartitionSpec as P

NT = 2048
PERIODS = 40

damping = 0.05
sample_step = 0.1

LANES = 128
STRAINS = 6
BLOCK = 4
GROUP = 16
BF16 = jnp.bfloat16
F32 = jnp.float32


def basis_angles(freq_count, sample_count, fine):
    freq_ids = jnp.arange(freq_count, dtype=jnp.int32)
    tables = []
    for time_ids in (jnp.arange(0, sample_count, fine), jnp.arange(fine)):
        angles = (time_ids.astype(jnp.int32)[:, None] * freq_ids[None, :] % sample_count).astype(
            F32
        ) * (2.0 * math.pi / sample_count)
        tables += [jnp.cos(angles), jnp.sin(angles)]
    return tables


def oscillator_gains(period_count, freq_count, sample_count):
    period_ids = jnp.arange(period_count, dtype=F32)
    periods = 2.0 * jnp.exp(period_ids * (math.log(5.0) / max(period_count - 1, 1)))
    natural = 2.0 * math.pi / periods
    omega_bins = jnp.arange(freq_count, dtype=F32) * (2.0 * math.pi / (sample_count * sample_step))
    squared_natural = (natural * natural)[:, None]
    real_part = squared_natural - (omega_bins * omega_bins)[None, :]
    imag_part = 2.0 * damping * natural[:, None] * omega_bins[None, :]
    magnitude = real_part * real_part + imag_part * imag_part
    return (-squared_natural * real_part / magnitude, squared_natural * imag_part / magnitude)


def roll_groups(array, groups, count):
    shift = (groups % count) * (LANES // count)
    return pltpu.roll(array, shift, 1) if shift else array


def swap_blocks(parts):
    count = len(parts)
    group = lax.broadcasted_iota(jnp.int32, parts[0].shape, 1) // (LANES // count)
    step = 1
    while step < count:
        own = (group & step) == 0
        parts = [jnp.where(own, parts[i], parts[(i + step) % count]) for i in range(count)]
        step *= 2
    return [parts[-d % count] for d in range(count)]


def pack_slip_kernel(workers, slip_hbm, mech_hbm, out_hbm, narrow, mech_ref, out_ref, wide, padded, done, mech_done, sent):
    core = lax.rem(lax.axis_index("site"), 2)
    stride = 2 * workers
    slots = mech_ref.shape[1]
    rows = out_ref.shape[1] - slots
    tall = rows // slots
    block = slip_hbm.shape[0] // slots
    pieces = done.shape[0]
    height = rows // pieces
    copies = []
    for i in range(pieces):
        here = pl.ds(i * height * stride, height * stride)
        copies.append(pltpu.make_async_copy(slip_hbm.at[here, :], narrow.at[here, :], done.at[i]))
        copies[i].start()
    mech_copy = pltpu.make_async_copy(mech_hbm, mech_ref, mech_done)
    mech_copy.start()
    padded[...] = jnp.zeros_like(padded)
    mech_copy.wait()
    padded[:STRAINS, :slots] = mech_ref[...]
    moments = padded[...].T[:slots, :]
    first = moments.astype(BF16).astype(F32)
    second = (moments - first).astype(BF16).astype(F32)
    third = moments - first - second
    coded = (
        first + pltpu.roll(second, STRAINS, 1) + pltpu.roll(third, 2 * STRAINS, 1)
    ).astype(BF16)
    for d in range(workers):
        out_ref[d, rows:, :] = coded
    sends = [
        pltpu.make_async_copy(out_ref.at[:, part, :], out_hbm.at[:, part, :], sent.at[i])
        for i, part in enumerate(
            [pl.ds(i * height, height) for i in range(pieces)] + [pl.ds(rows, slots)]
        )
    ]
    sends[pieces].start()
    chunk = 16
    for i in range(pieces):
        copies[i].wait()
        here = pl.ds(i * height * stride, height * stride)
        wide[here, :] = narrow[here, :].astype(F32)
        for start in range(i * height, (i + 1) * height, chunk):
            first = start // tall
            parts = []
            for x in range(workers):
                lines = [
                    wide[pl.ds(j * block + 2 * x * tall + core, tall, stride=2), :]
                    for j in range(first, first + chunk // tall)
                ]
                parts.append(
                    roll_groups(jnp.concatenate(lines, axis=0).astype(BF16), x, workers)
                )
            for d, part in enumerate(swap_blocks(parts)):
                out_ref[d, start : start + chunk, :] = part
        sends[i].start()
    for send in sends:
        send.wait()


def choose_kernel(
    workers, tall, high, point_ref, slots_ref, count_ref, chosen_ref, start_ref, line_ref
):
    points, total = chosen_ref.shape
    slots = total // workers
    point_ids = lax.axis_index("sub") * points + lax.broadcasted_iota(
        jnp.int32, (points, total), 0
    )
    chosen_ref[...] = (point_ref[...] == point_ids).astype(F32)

    def note_worker(w, filled):
        def note_slot(k, carry):
            j = w * slots + k
            start_ref[filled + k] = slots_ref[j] * high
            line_ref[filled + k] = j * tall
            return carry

        count = count_ref[w]
        lax.fori_loop(0, count, note_slot, 0)
        return filled + count

    amount = lax.fori_loop(0, workers, note_worker, 0)
    for extra in range(GROUP):
        start_ref[amount + extra] = 0
        line_ref[amount + extra] = 0
    start_ref[total + GROUP] = (amount + 2 * BLOCK - 1) // (2 * BLOCK)
    line_ref[total + GROUP] = amount


def project_kernel(
    workers, chosen_ref, recv_ref, sgt_ref, out_hbm, out_ref, moments, wide, sent
):
    points = sgt_ref.shape[0]
    sites = sgt_ref.shape[4]
    mech_start = recv_ref.shape[1] - chosen_ref.shape[1] // workers
    coded = jnp.concatenate([recv_ref[w, mech_start:, :] for w in range(workers)], axis=0)
    coded = jnp.dot(chosen_ref[...], coded, preferred_element_type=F32)
    moments[...] = (
        coded + pltpu.roll(coded, LANES - STRAINS, 1) + pltpu.roll(coded, LANES - 2 * STRAINS, 1)
    )
    height = 4 * sites

    def one_point(row):
        moment = moments[pl.ds(row, 1), :]
        weights = [
            jnp.broadcast_to(moment[:, m : m + 1], (sites, LANES)) for m in range(STRAINS)
        ]
        for p in range(2):
            for c in range(2):
                combined = weights[0] * sgt_ref[row, p, c, 0].astype(F32)
                for m in range(1, STRAINS):
                    combined = combined + weights[m] * sgt_ref[row, p, c, m].astype(F32)
                start = pl.multiple_of(row * height + (2 * p + c) * sites, sites)
                wide[pl.ds(start, sites), :] = combined.astype(BF16).astype(F32)

    rows = out_ref.shape[1]
    pieces = sent.shape[0]
    group = 4
    chunk = 16

    def some_points(step, carry):
        for u in range(group):
            one_point(step * group + u)
        return carry

    sends = []
    for i in range(pieces):
        steps = points // pieces // group
        if steps == 1:
            some_points(i, 0)
        else:
            lax.fori_loop(i * steps, (i + 1) * steps, some_points, 0)
        for start in range(i * rows // pieces, (i + 1) * rows // pieces, chunk):
            parts = [
                roll_groups(
                    wide[pl.ds(start * workers + x, chunk, stride=workers), :].astype(BF16),
                    x,
                    workers,
                )
                for x in range(workers)
            ]
            for d, part in enumerate(swap_blocks(parts)):
                out_ref[d, start : start + chunk, :] = part
        here = pl.ds(i * rows // pieces, rows // pieces)
        sends.append(
            pltpu.make_async_copy(out_ref.at[:, here, :], out_hbm.at[:, here, :], sent.at[i])
        )
        sends[i].start()
    for send in sends:
        send.wait()


def gather_kernel(workers, tall, line_ref, own_ref, other_ref, spread_ref, slip, wide):
    core = lax.rem(lax.axis_index("site"), 2)
    total = line_ref.shape[0] - GROUP - 1
    amount = line_ref[total + GROUP]
    slip_rows = total // workers * tall
    height = workers * tall
    for w in range(workers):
        here = slice(w * slip_rows, (w + 1) * slip_rows)
        slip[core, here, :] = own_ref[w, :slip_rows, :].astype(F32)
        slip[1 - core, here, :] = other_ref[w, :slip_rows, :].astype(F32)
    width = LANES // workers
    me = lax.axis_index("sub")
    group = lax.broadcasted_iota(jnp.int32, (tall, LANES), 1) // width
    row_ids = lax.broadcasted_iota(jnp.int32, (LANES, LANES), 0)
    lane_ids = lax.broadcasted_iota(jnp.int32, (LANES, LANES), 1)
    repeat = (row_ids % width == lane_ids % width).astype(F32).astype(BF16)

    def spread_slots(step, carry):
        for i in range(GROUP):
            index = step * GROUP + i
            for p in range(2):
                packed = slip[p, pl.ds(pl.multiple_of(line_ref[index], tall), tall), :]
                for x in range(workers):
                    wide[i, p, x * tall : (x + 1) * tall, :] = jnp.where(
                        (group == lax.rem(x + me, workers)) & (index < amount), packed, 0.0
                    )
        for i in range(GROUP):
            start = pl.multiple_of((step * GROUP + i) * height, height)
            for p in range(2):
                spread_ref[p, pl.ds(start, height), :] = jnp.dot(
                    wide[i, p].astype(BF16), repeat, preferred_element_type=F32
                ).astype(BF16)
        return carry

    lax.fori_loop(0, (amount + GROUP - 1) // GROUP, spread_slots, 0)


def contract_kernel(
    workers, tall, start_ref, spread_ref, proj_ref, out_ref, proj, even, odd, total, outgoing
):
    proj_rows = proj_ref.shape[1]
    high = outgoing.shape[0] // (workers * tall)
    half = high // 2
    variations = workers * tall
    lines = min(2, half)
    for w in range(workers):
        proj[w * proj_rows : (w + 1) * proj_rows, :] = proj_ref[w].astype(F32)
    total[...] = jnp.zeros_like(total)

    def widen_block(first, spread):
        for i in range(BLOCK):
            here = pl.ds(pl.multiple_of((first + i) * variations, variations), variations)
            real = spread_ref[0, here, :].astype(F32)
            imag = spread_ref[1, here, :].astype(F32)
            spread[0, i] = real + imag
            spread[1, i] = imag
            spread[2, i] = real

    def add_block(first, spread):
        starts = [start_ref[first + i] for i in range(BLOCK)]
        for line in range(0, half, lines):
            green = []
            for i in range(BLOCK):
                for y in range(line, line + lines):
                    real = jnp.broadcast_to(proj[pl.ds(starts[i] + y, 1), :], (tall, LANES))
                    imag = jnp.broadcast_to(proj[pl.ds(starts[i] + half + y, 1), :], (tall, LANES))
                    green.append((real, real + imag, imag - real))
            for x in range(workers):
                sums = [
                    [total[kind, y, x] for kind in range(3)] for y in range(line, line + lines)
                ]
                for i in range(BLOCK):
                    factors = [spread[kind, i, x * tall : (x + 1) * tall, :] for kind in range(3)]
                    for y in range(lines):
                        for kind in range(3):
                            sums[y][kind] = (
                                sums[y][kind] + green[i * lines + y][kind] * factors[kind]
                            )
                for y in range(lines):
                    for kind in range(3):
                        total[kind, line + y, x] = sums[y][kind]

    def add_two_blocks(step, carry):
        first = step * (2 * BLOCK)
        widen_block(first, even)
        widen_block(first + BLOCK, odd)
        add_block(first, even)
        add_block(first + BLOCK, odd)
        return carry

    lax.fori_loop(0, start_ref[start_ref.shape[0] - 1], add_two_blocks, 0)
    for y in range(half):
        for x in range(workers):
            shared = total[0, y, x]
            at_real = (x * high + y) * tall
            at_imag = (x * high + half + y) * tall
            outgoing[at_real : at_real + tall, :] = shared - total[1, y, x]
            outgoing[at_imag : at_imag + tall, :] = shared + total[2, y, x]
    out_ref[...] = outgoing[...].astype(BF16)


def dot_rows(a, b):
    return lax.dot_general(a, b, (((1,), (1,)), ((), ())), preferred_element_type=F32)


def tables_kernel(
    coarse_cos_ref, coarse_sin_ref, fine_cos_ref, fine_sin_ref, ready_hbm, basis_ref, rest_ref
):
    del ready_hbm
    fine, freqs = fine_cos_ref.shape
    norm_scale = 1.0 / math.sqrt(freqs)
    cosine = norm_scale * fine_cos_ref[...]
    sine = norm_scale * fine_sin_ref[...]
    for i in range(coarse_cos_ref.shape[0]):
        start_cos, start_sin = coarse_cos_ref[i : i + 1, :], coarse_sin_ref[i : i + 1, :]
        here = slice(i * fine, (i + 1) * fine)
        for part, values in enumerate(
            (start_cos * cosine - start_sin * sine, -(start_sin * cosine) - start_cos * sine)
        ):
            low = values.astype(BF16)
            basis_ref[here, part * freqs : (part + 1) * freqs] = low
            rest_ref[here, part * freqs : (part + 1) * freqs] = (
                values - low.astype(F32)
            ).astype(BF16)


def synthesis_kernel(
    workers,
    tall,
    recv_ref,
    gain_re_ref,
    gain_im_ref,
    basis_ref,
    rest_ref,
    motion_hbm,
    peak_ref,
    received,
    natural,
    peaks,
    motion_ref,
    done,
):
    freqs = natural.shape[1]
    rows = recv_ref.shape[0] // workers
    high = rows // tall
    if rows % 16:
        received[...] = recv_ref[...].astype(F32)
        parts = [received[w * rows : (w + 1) * rows, :] for w in range(workers)]
    else:
        parts = [recv_ref[w * rows : (w + 1) * rows, :] for w in range(workers)]
    for x, part in enumerate(swap_blocks(parts)):
        part = roll_groups(part, -x, workers).astype(F32)
        for r in range(high):
            start = (r * workers + x) * tall
            natural[start : start + tall, :] = part[r * tall : (r + 1) * tall, :]
    real, imag = [
        jnp.concatenate(
            [
                natural[pl.ds(r * workers * tall + v, workers, stride=tall), :]
                for v in range(tall)
                for r in range(first, first + high // 2)
            ],
            axis=0,
        )
        for first in (0, high // 2)
    ]
    spectrum = jnp.concatenate([real.astype(BF16), imag.astype(BF16)], axis=1)
    samples = basis_ref.shape[0]
    tile = samples // 4
    copies = []
    for i in range(4):
        here = slice(i * tile, (i + 1) * tile)
        motion = dot_rows(spectrum, basis_ref[here, :]) + dot_rows(spectrum, rest_ref[here, :])
        motion_ref[:, here] = motion.astype(BF16)
        copies.append(
            pltpu.make_async_copy(motion_ref.at[:, here], motion_hbm.at[:, here], done.at[i])
        )
        copies[i].start()

    def response_of(q):
        gain_re = gain_re_ref[q : q + 1, :]
        gain_im = gain_im_ref[q : q + 1, :]
        return jnp.concatenate(
            [
                (gain_re * real - gain_im * imag).astype(BF16),
                (gain_re * imag + gain_im * real).astype(BF16),
            ],
            axis=1,
        )

    def some_periods(first, number):
        response = jnp.concatenate([response_of(first + i) for i in range(number)], axis=0)
        peak = None
        for t in range(0, samples, tile):
            wave = jnp.abs(dot_rows(basis_ref[t : t + tile, :], response))
            wave = jnp.max(wave.reshape(tile // 8, 8, wave.shape[1]), axis=0)
            peak = wave if peak is None else jnp.maximum(peak, wave)
        top = jnp.max(peak, axis=0, keepdims=True)
        columns = top.shape[1] // number
        for i in range(number):
            peaks[first + i : first + i + 1, :] = top[:, i * columns : (i + 1) * columns]

    periods = gain_re_ref.shape[0]
    together = 2
    for first in range(0, periods, together):
        some_periods(first, min(together, periods - first))
    peak_ref[...] = peaks[...].T[:, :periods]
    for copy in copies:
        copy.wait()


def vmem():
    return pl.BlockSpec(memory_space=pltpu.VMEM)


def hbm():
    return pl.BlockSpec(memory_space=pltpu.HBM)


def smem():
    return pl.BlockSpec(memory_space=pltpu.SMEM)


def params(mebibytes, held=0):
    return pltpu.CompilerParams(vmem_limit_bytes=mebibytes * 2**20 + held)


def beside(microseconds):
    return pl.CostEstimate(
        flops=microseconds * 10**9, bytes_accessed=microseconds * 3 * 10**6, transcendentals=0
    )


def per_device(sgt, mechanism, slip, point_list, subfault_counts):
    workers = lax.axis_size("sub")
    site_parts = lax.axis_size("site")
    slots, variations, _, freqs = slip.shape
    points, _, components, _, sites, _ = sgt.shape
    total = point_list.shape[0]
    tall = variations // workers
    high = 2 * components * sites // workers
    slip_rows = slots * tall
    proj_rows = points * high
    flat = slip.reshape(slots * variations * 2, freqs)
    packed = pl.pallas_call(
        functools.partial(pack_slip_kernel, workers),
        out_shape=jax.ShapeDtypeStruct((workers, slip_rows + slots, LANES), BF16),
        in_specs=[hbm(), hbm()],
        out_specs=hbm(),
        scratch_shapes=[
            pltpu.VMEM(flat.shape, BF16),
            pltpu.VMEM((STRAINS, slots), F32),
            pltpu.VMEM((workers, slip_rows + slots, LANES), BF16),
            pltpu.VMEM((flat.shape[0] + 2 * tall, freqs), F32),
            pltpu.VMEM((LANES, LANES), F32),
            pltpu.SemaphoreType.DMA((8,)),
            pltpu.SemaphoreType.DMA,
            pltpu.SemaphoreType.DMA((9,)),
        ],
        compiler_params=params(58),
        name="pack_slip",
    )(flat, mechanism.T)
    own = lax.all_to_all(packed, "sub", split_axis=0, concat_axis=0, tiled=True)
    other = lax.ppermute(own, "site", [(i, i ^ 1) for i in range(site_parts)])
    chosen, starts, lines = pl.pallas_call(
        functools.partial(choose_kernel, workers, tall, high),
        out_shape=(
            jax.ShapeDtypeStruct((points, total), F32),
            jax.ShapeDtypeStruct((total + GROUP + 1,), jnp.int32),
            jax.ShapeDtypeStruct((total + GROUP + 1,), jnp.int32),
        ),
        in_specs=[vmem(), smem(), smem()],
        out_specs=(vmem(), smem(), smem()),
        cost_estimate=beside(10),
        name="choose",
    )(point_list.reshape(1, total), point_list, subfault_counts)
    chosen = chosen.astype(BF16)
    projected = pl.pallas_call(
        functools.partial(project_kernel, workers),
        out_shape=jax.ShapeDtypeStruct((workers, proj_rows, LANES), BF16),
        in_specs=[vmem(), vmem(), vmem()],
        out_specs=hbm(),
        scratch_shapes=[
            pltpu.VMEM((workers, proj_rows, LANES), BF16),
            pltpu.VMEM((points, LANES), F32),
            pltpu.VMEM((proj_rows * workers + workers, LANES), F32),
            pltpu.SemaphoreType.DMA((4,)),
        ],
        compiler_params=params(24),
        name="project",
    )(chosen, own, sgt)
    chunks = lax.all_to_all(projected, "sub", split_axis=0, concat_axis=0, tiled=True)
    capacity = total // 2 + GROUP
    spread_bytes = 2 * capacity * variations * LANES * 2
    spread = pl.pallas_call(
        functools.partial(gather_kernel, workers, tall),
        out_shape=jax.ShapeDtypeStruct((2, capacity * variations, LANES), BF16),
        in_specs=[smem(), vmem(), vmem()],
        out_specs=vmem(),
        scratch_shapes=[
            pltpu.VMEM((2, workers * slip_rows, LANES), F32),
            pltpu.VMEM((GROUP, 2, variations, LANES), F32),
        ],
        compiler_params=params(16, spread_bytes),
        name="gather",
    )(lines, own, other)
    partial_rows = tall * high
    spectrum = pl.pallas_call(
        functools.partial(contract_kernel, workers, tall),
        out_shape=jax.ShapeDtypeStruct((workers * partial_rows, LANES), BF16),
        in_specs=[smem(), vmem(), vmem()],
        out_specs=vmem(),
        scratch_shapes=[
            pltpu.VMEM((workers * proj_rows, LANES), F32),
            pltpu.VMEM((3, BLOCK, variations, LANES), F32),
            pltpu.VMEM((3, BLOCK, variations, LANES), F32),
            pltpu.VMEM((3, high // 2, workers, tall, LANES), F32),
            pltpu.VMEM((high * variations, LANES), F32),
        ],
        compiler_params=params(12, spread_bytes),
        name="contract",
    )(starts, spread, chunks)
    basis, basis_rest = pl.pallas_call(
        tables_kernel,
        out_shape=(jax.ShapeDtypeStruct((NT, 2 * freqs), BF16),) * 2,
        in_specs=[vmem()] * 4 + [hbm()],
        out_specs=(vmem(), vmem()),
        compiler_params=params(16),
        name="tables",
    )(*basis_angles(freqs, NT, 64), spectrum)
    gains = oscillator_gains(PERIODS, freqs, NT)
    spectrum = lax.all_to_all(spectrum, "sub", split_axis=0, concat_axis=0, tiled=True)
    width = tall * components * sites
    motion, peaks = pl.pallas_call(
        functools.partial(synthesis_kernel, workers, tall),
        out_shape=(
            jax.ShapeDtypeStruct((width, NT), BF16),
            jax.ShapeDtypeStruct((width, PERIODS), F32),
        ),
        in_specs=[vmem()] * 5,
        out_specs=(hbm(), vmem()),
        scratch_shapes=[
            pltpu.VMEM(spectrum.shape, F32),
            pltpu.VMEM((2 * width + workers, freqs), F32),
            pltpu.VMEM((LANES, width), F32),
            pltpu.VMEM((width, NT), BF16),
            pltpu.SemaphoreType.DMA((4,)),
        ],
        compiler_params=params(32),
        name="synthesis",
    )(spectrum, *gains, basis, basis_rest)
    return (
        motion.reshape(tall, components, sites, NT),
        peaks.reshape(tall, components, sites, PERIODS),
    )


def solution(mesh):
    in_specs = (
        P("sub", None, None, None, "site", None),
        P("sub", None),
        P("sub", None, None, None),
        P(),
        P(),
    )
    out_specs = (P("sub", None, "site", None), P("sub", None, "site", None))
    return jax.shard_map(
        per_device, mesh=mesh, in_specs=in_specs, out_specs=out_specs, check_vma=False
    )
```
